128 devices in a mesh: band: 16 (over x, y), slab: 8 (over z, core).
Axes of the slice: x: 4, y: 4, z: 4, core: 2. Of those that a mesh axis runs over, the one named last changes fastest.
Arguments:
- orbitals: bfloat16 [2, 128, 64, 240, 128], P(None, ('band', 'slab')), may hold values from -6 to 6
- potential: float32 [8, 30, 16, 512], P('slab', None, 'band'), may hold values from -1.5 to 1.5
- projector: bfloat16 [8, 30, 16, 4, 64, 512], P('slab', None, 'band'), may hold values from -0.046875 to 0.046875
- block_group: int32 [8, 30, 16, 4], P('slab', None, 'band'), may hold values from 0 to 15, all different within a row
- strengths: float32 [128, 8, 8], replicated, may hold values from -4 to 4
Outputs:
- applied: bfloat16 [2, 128, 64, 240, 128], P(None, ('band', 'slab'))
The draws below stay inside these ranges and needn't reach their ends.
Inputs may be any that keep to these rules, and one draw needn't show every extreme that they name: `block_group`: the 4 entries of one brick name different atom groups; every group is named by some brick.
All inputs are finite; a program needn't handle non-finite values.
Results may differ from the reference program's by a relative error of at most 0.012.
Values may be sent and summed in bfloat16 or wider, within the bound.
No kernel may reach another device: no remote copies, remote signals or barrier semaphores. Data moves between devices by JAX's collectives and lax.ppermute only.
A program may use at most 256 MiB of HBM per device.

```python
import math
import jax
import jax.numpy as jnp
from jax import lax

X = 240
Y = 128
BE = 8
P_SIZE = 512
KB = 4
C = 64
PROJ = 8
NB = 128
NZB = 8
NZ = 64
XB = 30
YB = 16
NATOM = 128
NGROUP = 16


def block_levels(rng, dims, pieces, low, largest):
    level, own = 1.0, jax.random.fold_in(rng, 6)
    for position, shards_of in pieces:
        heights = jnp.exp(jax.random.uniform(jax.random.fold_in(own, position), (shards_of,), jnp.float32, low / len(pieces), largest / len(pieces)))
        level = level * jnp.repeat(heights, dims[position] // shards_of).reshape([-1 if axis == position else 1 for axis in range(len(dims))])
    return level


def different_ones(key, rows, number_of, top, lift):
    ranking = jax.random.permutation(jax.random.fold_in(key, 1), number_of)
    pull = ranking
    for power in range(3):
        pull = pull * pull // number_of
    pull = pull * lift // number_of
    lots = jax.random.randint(jax.random.fold_in(key, 2), (rows, number_of), 0, 4096) + pull
    holders = jax.random.permutation(jax.random.fold_in(key, 3), rows)[jnp.arange(number_of) % rows]
    lots = jnp.where(jnp.arange(rows)[:, None] == holders[None, :], 1 << 14, lots)
    score = lots * number_of + jnp.arange(number_of)
    return lax.top_k(score.astype(jnp.int32), top)[1].astype(jnp.int32)


def noise(rng, shape, deviation, limit, pieces=(), kind=jnp.bfloat16):
    values = jax.random.normal(rng, shape, jnp.float32) * deviation
    if len(pieces) > 0:
        values = block_levels(rng, shape, pieces, -0.22, 0.18) * values
    return jnp.clip(values, min=-limit, max=limit).astype(kind)


def setup_inputs(seed: int = 0) -> dict:
    key_list = jax.random.split(jax.random.key(seed), 6)
    orbitals = noise(key_list[0], (2, NB, NZ, X, Y), 1.0, 6.0, ((1, 128),))
    potential = jnp.clip(jax.random.uniform(key_list[1], (NZB, XB, YB, P_SIZE), jnp.float32, -1.5, 1.5) * block_levels(key_list[1], (NZB, XB, YB, P_SIZE), ((0, 8), (2, 16)), -0.4, 0.0), -1.5, 1.5)
    projector = noise(key_list[2], (NZB, XB, YB, KB, C, P_SIZE), (P_SIZE * C // 2) ** -0.5, 0.046875, ((0, 8), (2, 16)))
    block_group = different_ones(key_list[3], NZB * XB * YB, NGROUP, KB, 4096).reshape((NZB, XB, YB, KB))
    strengths = noise(key_list[4], (NATOM, PROJ, PROJ), 1.0, 4.0, (), jnp.float32)
    return dict(orbitals=orbitals, potential=potential, projector=projector, block_group=block_group, strengths=strengths)


KINETIC_SCALE = 8.0

def dft_table(length, orient):
    counter = jnp.arange(length, dtype=jnp.int32)
    product = counter[:, None] * counter[None, :] % length
    phases = product.astype(jnp.float32) * (2.0 * math.pi / length)
    cosine = jnp.cos(phases) / math.sqrt(length)
    sine_part = orient * jnp.sin(phases) / math.sqrt(length)
    return jnp.stack([jnp.stack([cosine, -sine_part]), jnp.stack([sine_part, cosine])]).astype(jnp.bfloat16)

def kinetic_term(spectrum):
    rows_x = spectrum.shape[-2]
    rows_y = spectrum.shape[-1]
    wave_x = jnp.arange(rows_x, dtype=jnp.int32)
    wave_x = jnp.minimum(wave_x, rows_x - wave_x).astype(jnp.float32) / rows_x
    wave_y = jnp.arange(rows_y, dtype=jnp.int32)
    wave_y = jnp.minimum(wave_y, rows_y - wave_y).astype(jnp.float32) / rows_y
    planar = KINETIC_SCALE * (wave_x[:, None] * wave_x[:, None] + wave_y[None, :] * wave_y[None, :])
    values = spectrum.astype(jnp.float32)
    widths = [(0, 0)] * (values.ndim - 3) + [(1, 1), (0, 0), (0, 0)]
    padded = jnp.pad(values, widths)
    along_z = 0.5 * (2.0 * values - padded[..., 2:, :, :] - padded[..., :-2, :, :])
    return planar * values + along_z

def reference(orbitals, potential, projector, block_group, strengths):
    inverse_y = dft_table(Y, 1.0).astype(jnp.float32)
    inverse_x = dft_table(X, 1.0).astype(jnp.float32)
    forward_x = dft_table(X, -1.0).astype(jnp.float32)
    forward_y = dft_table(Y, -1.0).astype(jnp.float32)
    shaped_proj = projector.reshape(-1, KB, C, P_SIZE).astype(jnp.float32)
    n_bricks = shaped_proj.shape[0]
    groups = block_group.reshape(n_bricks, KB)
    onehot = (groups[:, :, None] == jnp.arange(NGROUP, dtype=jnp.int32)[None, None, :]).astype(jnp.float32)
    symmetric = 0.5 * (strengths + jnp.transpose(strengths, (0, 2, 1)))
    pot_rows = potential.reshape(n_bricks, P_SIZE)
    blocked = orbitals.reshape(2, NB // 8, 8, NZ, X, Y).transpose(1, 0, 2, 3, 4, 5)
    highest = lax.Precision.HIGHEST

    def apply_block(spectrum):
        across_y = jnp.einsum('ibzxy,oiyk->obzxk', spectrum.astype(jnp.float32), inverse_y, precision=highest).astype(jnp.bfloat16)
        real_grid = jnp.einsum('ibzxy,oixk->obzky', across_y.astype(jnp.float32), inverse_x, precision=highest).astype(jnp.bfloat16)
        bricks = real_grid.reshape(2, 8, NZB, BE, XB, BE, YB, BE).transpose(1, 0, 2, 4, 6, 3, 5, 7).reshape(16, n_bricks, P_SIZE)
        partial_terms = jnp.einsum('rbq,bkpq->bkpr', bricks.astype(jnp.float32), shaped_proj, precision=highest)
        coefficient = jnp.einsum('bkpr,bkg->gpr', partial_terms, onehot, precision=highest)
        scaled = jnp.einsum('aji,ajr->air', symmetric, coefficient.reshape(NATOM, PROJ, 16), precision=highest).astype(jnp.bfloat16)
        picked = jnp.einsum('gpr,bkg->bkpr', scaled.reshape(NGROUP, C, 16).astype(jnp.float32), onehot, precision=highest).astype(jnp.bfloat16)
        projected = jnp.einsum('bkpr,bkpq->rbq', picked.astype(jnp.float32), shaped_proj, precision=highest)
        acted = (pot_rows[None] * bricks.astype(jnp.float32) + projected).astype(jnp.bfloat16)
        grid_back = acted.reshape(8, 2, NZB, XB, YB, BE, BE, BE).transpose(1, 0, 2, 5, 3, 6, 4, 7).reshape(2, 8, NZ, X, Y)
        halfway = jnp.einsum('ibzxy,oixk->obzky', grid_back.astype(jnp.float32), forward_x, precision=highest).astype(jnp.bfloat16)
        result = jnp.einsum('ibzxy,oiyk->obzxk', halfway.astype(jnp.float32), forward_y, precision=highest) + kinetic_term(spectrum)
        return result.astype(jnp.bfloat16)
    applied = lax.map(apply_block, blocked)
    return applied.transpose(1, 0, 2, 3, 4, 5).reshape(2, NB, NZ, X, Y)
```

```python
import math

import jax
import jax.numpy as jnp
import numpy as np
from jax import lax
from jax.experimental import pallas as pl
from jax.experimental.pallas import tpu as pltpu
from jax.sharding import PartitionSpec as P

X = 240
Y = 128
NZ = 64
BE = 8
P_SIZE = 512
KB = 4
C = 64
PROJ = 8
XB = X // BE
PAIRS = XB // 2
NBAND = 16
NSLAB = 8
NDEV = NBAND * NSLAB
NGROUP = 16
ROWS = 2 * NDEV
HALF = 64
KINETIC_SCALE = 8.0
AXES = ("band", "slab")
F32 = jnp.float32
BF16 = jnp.bfloat16
VMEM_LIMIT = 48 * 1024 * 1024


def cos_sin(length):
    counter = np.arange(length)
    phases = (counter[:, None] * counter[None, :] % length) * (2.0 * math.pi / length)
    return np.cos(phases) / math.sqrt(length), np.sin(phases) / math.sqrt(length)


def bf16_table(values):
    return jnp.asarray(np.asarray(values, np.float32), dtype=BF16)


def x_order():
    x = np.arange(X).reshape(XB, BE // 2, 2)
    return x.transpose(2, 0, 1).reshape(-1)


def point_order():
    q = np.arange(P_SIZE).reshape(BE, BE, BE)
    return q.transpose(1, 0, 2).reshape(-1)


def nt(a, b):
    return lax.dot_general(a, b, (((1,), (1,)), ((), ())), preferred_element_type=F32)


def nn(a, b):
    return lax.dot_general(a, b, (((1,), (0,)), ((), ())), preferred_element_type=F32)


def to_grid_kernel(spec_ref, ty_ref, tx_ref, out_ref, across_ref):
    for e in range(BE):
        plane = jnp.concatenate([spec_ref[0, 0, e], spec_ref[1, 0, e]], axis=1)
        across = nt(ty_ref[...], plane)
        across_ref[:, :, e] = across.reshape(2, NBAND, BE, X)
    low = lax.broadcasted_iota(jnp.int32, (X // 2, 128), 1) < HALF

    def column(c, carry):
        re = across_ref[0, c].reshape(BE * BE, X).astype(BF16)
        im = across_ref[1, c].reshape(BE * BE, X).astype(BF16)
        whole = nt(tx_ref[0], jnp.concatenate([re, im], axis=0)) + nt(
            tx_ref[1], jnp.concatenate([-im, re], axis=0)
        )
        even = whole[: X // 2]
        odd = whole[X // 2 :]
        first = jnp.where(low, even, pltpu.roll(odd, HALF, 1))
        second = jnp.where(low, pltpu.roll(even, HALF, 1), odd)
        rows = jnp.stack(
            [first.reshape(PAIRS, 8, 128), second.reshape(PAIRS, 8, 128)], axis=1
        ).reshape(X, 128)
        out_ref[c, 0] = rows.astype(BF16)
        return carry

    lax.fori_loop(0, NBAND, column, 0, unroll=2)


def to_grid(orbitals):
    cy, sy = cos_sin(Y)
    ty = bf16_table(np.block([[cy, -sy], [sy, cy]]))
    cx, sx = cos_sin(X)
    order = x_order()
    tx = bf16_table(np.stack([cx[order], sx[order]]))
    return pl.pallas_call(
        to_grid_kernel,
        grid=(NSLAB,),
        in_specs=[
            pl.BlockSpec((2, 1, BE, X, Y), lambda s: (0, 0, s, 0, 0)),
            pl.BlockSpec((2 * Y, 2 * Y), lambda s: (0, 0)),
            pl.BlockSpec((2, X, X), lambda s: (0, 0, 0)),
        ],
        out_specs=pl.BlockSpec((NBAND, 1, X, 128), lambda s: (0, s, 0, 0)),
        out_shape=jax.ShapeDtypeStruct((NBAND, NSLAB, X, 128), BF16),
        scratch_shapes=[pltpu.VMEM((2, NBAND, BE, BE, X), F32)],
        compiler_params=pltpu.CompilerParams(vmem_limit_bytes=VMEM_LIMIT),
        name="to_grid",
    )(orbitals, ty, tx)


def project_kernel(groups_ref, bricks_ref, proj_ref, rows_ref, sums_ref, wide_ref, coef_ref):
    t = pl.program_id(0)

    @pl.when(t == 0)
    def _():
        coef_ref[...] = jnp.zeros_like(coef_ref)

    wide_ref[...] = bricks_ref[...].astype(F32).reshape(NDEV * 16, 128)
    for low in range(2):
        for part in range(2):
            for high in range(4):
                j = part * 8 + low * 4 + high
                piece = wide_ref[pl.ds(j, NDEV, stride=16), :]
                rows_ref[low, pl.ds(part * NDEV, NDEV), pl.ds(high * 128, 128)] = piece.astype(BF16)
        partial = nt(proj_ref[low], rows_ref[low])
        for k in range(KB):
            g = groups_ref[(2 * t + low) * KB + k]
            coef_ref[g] += partial[k * C : (k + 1) * C]

    @pl.when(t == PAIRS - 1)
    def _():
        sums_ref[...] = coef_ref[...].astype(BF16)


def project(groups, bricks, proj):
    return pl.pallas_call(
        project_kernel,
        grid_spec=pltpu.PrefetchScalarGridSpec(
            num_scalar_prefetch=1,
            grid=(PAIRS,),
            in_specs=[
                pl.BlockSpec((NDEV, 16, 128), lambda t, g: (0, t, 0)),
                pl.BlockSpec((2, KB * C, P_SIZE), lambda t, g: (t, 0, 0)),
            ],
            out_specs=[
                pl.BlockSpec((2, ROWS, P_SIZE), lambda t, g: (t, 0, 0)),
                pl.BlockSpec((NGROUP, C, ROWS), lambda t, g: (0, 0, 0)),
            ],
            scratch_shapes=[
                pltpu.VMEM((NDEV * 16, 128), F32),
                pltpu.VMEM((NGROUP, C, ROWS), F32),
            ],
        ),
        out_shape=[
            jax.ShapeDtypeStruct((XB, ROWS, P_SIZE), BF16),
            jax.ShapeDtypeStruct((NGROUP, C, ROWS), BF16),
        ],
        compiler_params=pltpu.CompilerParams(vmem_limit_bytes=VMEM_LIMIT),
        name="project",
    )(groups, bricks, proj)


def couple_kernel(sums_ref, strength_ref, out_ref):
    total = jnp.sum(sums_ref[...].astype(F32), axis=0)
    strength = 0.5 * (strength_ref[0] + strength_ref[0].T)
    scaled = strength[:, 0:1] * total[0:1]
    for j in range(1, PROJ):
        scaled = scaled + strength[:, j : j + 1] * total[j : j + 1]
    out_ref[...] = jnp.broadcast_to(scaled[None], (NDEV, PROJ, ROWS)).astype(BF16)


def couple(sums, strengths):
    return pl.pallas_call(
        couple_kernel,
        out_shape=jax.ShapeDtypeStruct((NDEV, PROJ, ROWS), BF16),
        compiler_params=pltpu.CompilerParams(vmem_limit_bytes=VMEM_LIMIT),
        name="couple",
    )(sums, strengths)


def act_kernel(groups_ref, coupled_ref, rows_ref, proj_ref, pot_ref, out_ref, picks_ref, wide_ref):
    t = pl.program_id(0)

    @pl.when(t == 0)
    def _():
        unit = (
            lax.broadcasted_iota(jnp.int32, (ROWS, ROWS), 0)
            == lax.broadcasted_iota(jnp.int32, (ROWS, ROWS), 1)
        ).astype(BF16)
        zeros = jnp.zeros((C, ROWS), BF16)
        for g in range(NGROUP):
            block = coupled_ref[g]
            picks_ref[0, g] = nt(unit, jnp.concatenate([block, zeros], axis=0)).astype(BF16)
            picks_ref[1, g] = nt(unit, jnp.concatenate([zeros, block], axis=0)).astype(BF16)

    for low in range(2):
        g = [groups_ref[(2 * t + low) * KB + k] for k in range(KB)]
        picked = jnp.concatenate(
            [picks_ref[0, g[0]] + picks_ref[1, g[1]], picks_ref[0, g[2]] + picks_ref[1, g[3]]],
            axis=1,
        )
        acted = nn(picked, proj_ref[low]) + pot_ref[low] * rows_ref[low].astype(F32)
        for part in range(2):
            for high in range(4):
                j = part * 8 + low * 4 + high
                wide_ref[pl.ds(j, NDEV, stride=16), :] = acted[
                    part * NDEV : (part + 1) * NDEV, high * 128 : (high + 1) * 128
                ]
    out_ref[...] = wide_ref[...].reshape(NDEV, 16, 128).astype(BF16)


def act(groups, coupled, rows, proj, pot):
    return pl.pallas_call(
        act_kernel,
        grid_spec=pltpu.PrefetchScalarGridSpec(
            num_scalar_prefetch=1,
            grid=(PAIRS,),
            in_specs=[
                pl.BlockSpec((NGROUP, C, ROWS), lambda t, g: (0, 0, 0)),
                pl.BlockSpec((2, ROWS, P_SIZE), lambda t, g: (t, 0, 0)),
                pl.BlockSpec((2, KB * C, P_SIZE), lambda t, g: (t, 0, 0)),
                pl.BlockSpec((2, 1, P_SIZE), lambda t, g: (t, 0, 0)),
            ],
            out_specs=pl.BlockSpec((NDEV, 16, 128), lambda t, g: (0, t, 0)),
            scratch_shapes=[
                pltpu.VMEM((2, NGROUP, ROWS, 2 * C), BF16),
                pltpu.VMEM((NDEV * 16, 128), F32),
            ],
        ),
        out_shape=jax.ShapeDtypeStruct((NDEV, X, 128), BF16),
        compiler_params=pltpu.CompilerParams(vmem_limit_bytes=VMEM_LIMIT),
        name="act",
    )(groups, coupled, rows, proj, pot)


def to_waves_kernel(
    grid_ref, spec_ref, below_ref, above_ref, unit_ref, tx_ref, ty_ref, planar_ref, out_ref, turned_ref
):
    s = pl.program_id(0)

    def turn(c, carry):
        turned = nt(unit_ref[...], grid_ref[c, 0])
        turned_ref[:, :, c] = turned.reshape(2, BE, BE, X)
        return carry

    lax.fori_loop(0, NBAND, turn, 0, unroll=2)
    has_below = (s > 0).astype(F32)
    has_above = (s < NSLAB - 1).astype(F32)
    for e in range(BE):
        even = turned_ref[0, e].reshape(Y, X).astype(BF16)
        odd = turned_ref[1, e].reshape(Y, X).astype(BF16)
        half = nt(tx_ref[0], even) + nt(tx_ref[1], odd)
        half = jnp.concatenate([half[:X], half[X:]], axis=1).astype(BF16)
        result = nn(half, ty_ref[...])
        for o in range(2):
            here = spec_ref[o, 0, e].astype(F32)
            if e == 0:
                below = below_ref[o, 0, 0].astype(F32) * has_below
            else:
                below = spec_ref[o, 0, e - 1].astype(F32)
            if e == BE - 1:
                above = above_ref[o, 0, 0].astype(F32) * has_above
            else:
                above = spec_ref[o, 0, e + 1].astype(F32)
            kinetic = planar_ref[...] * here + 0.5 * (2.0 * here - above - below)
            out_ref[o, 0, e] = (result[:, o * Y : (o + 1) * Y] + kinetic).astype(BF16)


def to_waves(grid, orbitals):
    cx, sx = cos_sin(X)
    x = np.arange(X).reshape(PAIRS, 2, BE // 2, 2)
    tables = []
    for low in range(2):
        own = x[..., low].reshape(PAIRS, 8)
        re, im = np.zeros((2 * X, PAIRS, 8)), np.zeros((2 * X, PAIRS, 8))
        re[:X], re[X:] = cx[:, own], -sx[:, own]
        im[:X], im[X:] = sx[:, own], cx[:, own]
        tables.append(np.stack([re, im], axis=2).reshape(2 * X, X))
    tx = bf16_table(np.stack(tables))
    cy, sy = cos_sin(Y)
    ty = bf16_table(np.block([[cy, -sy], [sy, cy]]))
    wave_x = np.minimum(np.arange(X), X - np.arange(X)).astype(np.float32) / X
    wave_y = np.minimum(np.arange(Y), Y - np.arange(Y)).astype(np.float32) / Y
    planar = jnp.asarray(
        KINETIC_SCALE * (wave_x[:, None] * wave_x[:, None] + wave_y[None, :] * wave_y[None, :]), dtype=F32
    )
    return pl.pallas_call(
        to_waves_kernel,
        grid=(NSLAB,),
        in_specs=[
            pl.BlockSpec((NBAND, 1, X, 128), lambda s: (0, s, 0, 0)),
            pl.BlockSpec((2, 1, BE, X, Y), lambda s: (0, 0, s, 0, 0)),
            pl.BlockSpec((2, 1, 1, X, Y), lambda s: (0, 0, jnp.maximum(s * BE - 1, 0), 0, 0)),
            pl.BlockSpec((2, 1, 1, X, Y), lambda s: (0, 0, jnp.minimum(s * BE + BE, NZ - 1), 0, 0)),
            pl.BlockSpec((128, 128), lambda s: (0, 0)),
            pl.BlockSpec((2, 2 * X, X), lambda s: (0, 0, 0)),
            pl.BlockSpec((2 * Y, 2 * Y), lambda s: (0, 0)),
            pl.BlockSpec((X, Y), lambda s: (0, 0)),
        ],
        out_specs=pl.BlockSpec((2, 1, BE, X, Y), lambda s: (0, 0, s, 0, 0)),
        out_shape=jax.ShapeDtypeStruct((2, 1, NZ, X, Y), BF16),
        scratch_shapes=[pltpu.VMEM((2, BE, NBAND, BE, X), F32)],
        compiler_params=pltpu.CompilerParams(vmem_limit_bytes=VMEM_LIMIT),
        name="to_waves",
    )(grid, orbitals, orbitals, orbitals, bf16_table(np.eye(128)), tx, ty, planar)


def exchange(array):
    return lax.all_to_all(array, AXES, split_axis=0, concat_axis=0, tiled=True)


def on_device(orbitals, potential, projector, block_group, strengths):
    groups = block_group.reshape(-1)
    order = point_order()
    turn = np.zeros((P_SIZE, P_SIZE), np.float32)
    turn[order, np.arange(P_SIZE)] = 1.0
    proj = nn(projector.reshape(XB * KB * C, P_SIZE), jnp.asarray(turn, dtype=BF16)).astype(BF16)
    proj = proj.reshape(XB, KB * C, P_SIZE)
    pot = potential.reshape(XB, BE, BE, BE).transpose(0, 2, 1, 3).reshape(XB, 1, P_SIZE)
    own = lax.axis_index(AXES)
    strength = lax.dynamic_slice_in_dim(strengths, own, 1, 0)

    bricks = exchange(to_grid(orbitals).reshape(NDEV, X, 128))
    rows, sums = project(groups, bricks, proj)
    coupled = exchange(couple(exchange(sums.reshape(NDEV, PROJ, ROWS)), strength))
    acted = act(groups, coupled.reshape(NGROUP, C, ROWS), rows, proj, pot)
    returned = exchange(acted).reshape(NBAND, NSLAB, X, 128)
    return to_waves(returned, orbitals)


def solution(mesh):
    in_specs = (
        P(None, AXES, None, None, None),
        P("slab", None, "band", None),
        P("slab", None, "band", None, None, None),
        P("slab", None, "band", None),
        P(),
    )
    out_specs = P(None, AXES, None, None, None)
    return jax.shard_map(
        on_device, mesh=mesh, in_specs=in_specs, out_specs=out_specs, check_vma=False
    )
```

```python
import math

import jax
import jax.numpy as jnp
import numpy as np
from jax import lax
from jax.experimental import pallas as pl
from jax.experimental.pallas import tpu as pltpu
from jax.sharding import PartitionSpec as P

X = 240
Y = 128
NZ = 64
BE = 8
P_SIZE = 512
KB = 4
C = 64
PROJ = 8
XB = X // BE
PAIRS = XB // 2
NBAND = 16
NSLAB = 8
NDEV = NBAND * NSLAB
NGROUP = 16
ROWS = 2 * NDEV
HALF = 64
STEP = 3
PLANES = 4
KINETIC_SCALE = 8.0
AXES = ("band", "slab")
F32 = jnp.float32
BF16 = jnp.bfloat16
VMEM_LIMIT = 48 * 1024 * 1024


def cos_sin(length):
    counter = np.arange(length)
    phases = (counter[:, None] * counter[None, :] % length) * (2.0 * math.pi / length)
    return np.cos(phases) / math.sqrt(length), np.sin(phases) / math.sqrt(length)


def bf16_table(values):
    return jnp.asarray(np.asarray(values, np.float32), dtype=BF16)


def x_order():
    x = np.arange(X).reshape(XB, BE // 2, 2)
    return x.transpose(2, 0, 1).reshape(-1)


def point_order():
    q = np.arange(P_SIZE).reshape(BE, BE, BE)
    return q.transpose(1, 0, 2).reshape(-1)


def nt(a, b):
    return lax.dot_general(a, b, (((1,), (1,)), ((), ())), preferred_element_type=F32)


def nn(a, b):
    return lax.dot_general(a, b, (((1,), (0,)), ((), ())), preferred_element_type=F32)


def to_grid_kernel(spec_ref, ty_ref, tx_ref, out_ref, across_ref):
    for e in range(BE):
        plane = jnp.concatenate([spec_ref[0, 0, e], spec_ref[1, 0, e]], axis=1)
        across = nt(ty_ref[...], plane)
        across_ref[:, :, e] = across.reshape(2, NBAND, BE, X)
    low = lax.broadcasted_iota(jnp.int32, (X // 2, 128), 1) < HALF
    for c in range(0, NBAND, 2):
        re = [across_ref[0, c + i].reshape(BE * BE, X).astype(BF16) for i in range(2)]
        im = [across_ref[1, c + i].reshape(BE * BE, X).astype(BF16) for i in range(2)]
        whole = nt(tx_ref[0], jnp.concatenate([re[0], im[0], re[1], im[1]], axis=0)) + nt(
            tx_ref[1], jnp.concatenate([-im[0], re[0], -im[1], re[1]], axis=0)
        )
        for i in range(2):
            even = whole[: X // 2, i * 128 : (i + 1) * 128]
            odd = whole[X // 2 :, i * 128 : (i + 1) * 128]
            first = jnp.where(low, even, pltpu.roll(odd, HALF, 1))
            second = jnp.where(low, pltpu.roll(even, HALF, 1), odd)
            rows = jnp.stack(
                [first.reshape(PAIRS, 8, 128), second.reshape(PAIRS, 8, 128)], axis=1
            ).reshape(X, 128)
            out_ref[c + i, 0] = rows.astype(BF16)


def to_grid(orbitals):
    cy, sy = cos_sin(Y)
    ty = bf16_table(np.block([[cy, -sy], [sy, cy]]))
    cx, sx = cos_sin(X)
    order = x_order()
    tx = bf16_table(np.stack([cx[order], sx[order]]))
    return pl.pallas_call(
        to_grid_kernel,
        grid=(NSLAB,),
        in_specs=[
            pl.BlockSpec((2, 1, BE, X, Y), lambda s: (0, 0, s, 0, 0)),
            pl.BlockSpec((2 * Y, 2 * Y), lambda s: (0, 0)),
            pl.BlockSpec((2, X, X), lambda s: (0, 0, 0)),
        ],
        out_specs=pl.BlockSpec((NBAND, 1, X, 128), lambda s: (0, s, 0, 0)),
        out_shape=jax.ShapeDtypeStruct((NBAND, NSLAB, X, 128), BF16),
        scratch_shapes=[pltpu.VMEM((2, NBAND, BE, BE, X), F32)],
        compiler_params=pltpu.CompilerParams(vmem_limit_bytes=VMEM_LIMIT),
        name="to_grid",
    )(orbitals, ty, tx)


def turned_rows(bricks_ref, pair):
    turned = jnp.swapaxes(bricks_ref[:, pair * 16 : (pair + 1) * 16], 0, 1)
    return [
        jnp.concatenate(
            [
                jnp.concatenate([turned[part * 8 + low * 4 + high] for high in range(4)], axis=1)
                for part in range(2)
            ],
            axis=0,
        )
        for low in range(2)
    ]


def project_kernel(groups_ref, bricks_ref, proj_ref, sums_ref, coef_ref):
    t = pl.program_id(0)

    @pl.when(t == 0)
    def _():
        coef_ref[...] = jnp.zeros_like(coef_ref)

    for pair in range(STEP):
        rows = turned_rows(bricks_ref, pair)
        for low in range(2):
            b = 2 * pair + low
            partial = nt(proj_ref[b], rows[low])
            for k in range(KB):
                g = groups_ref[(2 * STEP * t + b) * KB + k]
                coef_ref[g] += partial[k * C : (k + 1) * C]

    @pl.when(t == PAIRS // STEP - 1)
    def _():
        sums_ref[...] = coef_ref[...].astype(BF16)


def project(groups, bricks, proj):
    return pl.pallas_call(
        project_kernel,
        grid_spec=pltpu.PrefetchScalarGridSpec(
            num_scalar_prefetch=1,
            grid=(PAIRS // STEP,),
            in_specs=[
                pl.BlockSpec((NDEV, 16 * STEP, 128), lambda t, g: (0, t, 0)),
                pl.BlockSpec((2 * STEP, KB * C, P_SIZE), lambda t, g: (t, 0, 0)),
            ],
            out_specs=pl.BlockSpec((NGROUP, C, ROWS), lambda t, g: (0, 0, 0)),
            scratch_shapes=[pltpu.VMEM((NGROUP, C, ROWS), F32)],
        ),
        out_shape=jax.ShapeDtypeStruct((NGROUP, C, ROWS), BF16),
        compiler_params=pltpu.CompilerParams(vmem_limit_bytes=VMEM_LIMIT),
        name="project",
    )(groups, bricks, proj)


def couple_kernel(sums_ref, strength_ref, out_ref):
    total = jnp.sum(sums_ref[...].astype(F32), axis=0)
    strength = 0.5 * (strength_ref[0] + strength_ref[0].T)
    scaled = strength[:, 0:1] * total[0:1]
    for j in range(1, PROJ):
        scaled = scaled + strength[:, j : j + 1] * total[j : j + 1]
    out_ref[...] = jnp.broadcast_to(scaled[None], (NDEV, PROJ, ROWS)).astype(BF16)


def couple(sums, strengths):
    return pl.pallas_call(
        couple_kernel,
        out_shape=jax.ShapeDtypeStruct((NDEV, PROJ, ROWS), BF16),
        compiler_params=pltpu.CompilerParams(vmem_limit_bytes=VMEM_LIMIT),
        name="couple",
    )(sums, strengths)


def act_kernel(groups_ref, coupled_ref, bricks_ref, proj_ref, pot_ref, out_ref, picks_ref):
    t = pl.program_id(0)

    @pl.when(t == 0)
    def _():
        unit = (
            lax.broadcasted_iota(jnp.int32, (ROWS, ROWS), 0)
            == lax.broadcasted_iota(jnp.int32, (ROWS, ROWS), 1)
        ).astype(BF16)
        zeros = jnp.zeros((C, ROWS), BF16)
        for g in range(NGROUP):
            block = coupled_ref[g]
            both = nt(unit, jnp.concatenate([block, zeros, zeros, block], axis=0)).astype(BF16)
            picks_ref[0, g] = both[:, : 2 * C]
            picks_ref[1, g] = both[:, 2 * C :]

    for pair in range(STEP):
        rows = turned_rows(bricks_ref, pair)
        pieces = [None] * 16
        for low in range(2):
            b = 2 * pair + low
            g = [groups_ref[(2 * STEP * t + b) * KB + k] for k in range(KB)]
            picked = jnp.concatenate(
                [picks_ref[0, g[0]] + picks_ref[1, g[1]], picks_ref[0, g[2]] + picks_ref[1, g[3]]],
                axis=1,
            )
            acted = nn(picked, proj_ref[b]) + pot_ref[b] * rows[low].astype(F32)
            acted = acted.astype(BF16)
            for part in range(2):
                for high in range(4):
                    pieces[part * 8 + low * 4 + high] = acted[
                        part * NDEV : (part + 1) * NDEV, high * 128 : (high + 1) * 128
                    ]
        out_ref[:, pair * 16 : (pair + 1) * 16] = jnp.swapaxes(jnp.stack(pieces), 0, 1)


def act(groups, coupled, bricks, proj, pot):
    return pl.pallas_call(
        act_kernel,
        grid_spec=pltpu.PrefetchScalarGridSpec(
            num_scalar_prefetch=1,
            grid=(PAIRS // STEP,),
            in_specs=[
                pl.BlockSpec((NGROUP, C, ROWS), lambda t, g: (0, 0, 0)),
                pl.BlockSpec((NDEV, 16 * STEP, 128), lambda t, g: (0, t, 0)),
                pl.BlockSpec((2 * STEP, KB * C, P_SIZE), lambda t, g: (t, 0, 0)),
                pl.BlockSpec((2 * STEP, 1, P_SIZE), lambda t, g: (t, 0, 0)),
            ],
            out_specs=pl.BlockSpec((NDEV, 16 * STEP, 128), lambda t, g: (0, t, 0)),
            scratch_shapes=[pltpu.VMEM((2, NGROUP, ROWS, 2 * C), BF16)],
        ),
        out_shape=jax.ShapeDtypeStruct((NDEV, X, 128), BF16),
        compiler_params=pltpu.CompilerParams(vmem_limit_bytes=VMEM_LIMIT),
        name="act",
    )(groups, coupled, bricks, proj, pot)


def to_waves_kernel(
    grid_ref, spec_ref, below_ref, above_ref, unit_ref, tx_ref, ty_ref, planar_ref, out_ref, turned_ref
):
    s = pl.program_id(0)

    for c in range(0, NBAND, 2):
        two = jnp.concatenate([grid_ref[c, 0], grid_ref[c + 1, 0]], axis=1)
        turned_ref[:, :, c : c + 2] = nt(unit_ref[...], two).reshape(2, BE, 2, BE, X)
    has_below = (s > 0).astype(F32)
    has_above = (s < NSLAB - 1).astype(F32)
    for first in range(0, BE, PLANES):
        even = turned_ref[0, first : first + PLANES].reshape(PLANES * Y, X).astype(BF16)
        odd = turned_ref[1, first : first + PLANES].reshape(PLANES * Y, X).astype(BF16)
        halves = nt(tx_ref[0], even) + nt(tx_ref[1], odd)
        for i in range(PLANES):
            e = first + i
            half = halves[:, i * Y : (i + 1) * Y]
            half = jnp.concatenate([half[:X], half[X:]], axis=1).astype(BF16)
            result = nn(half, ty_ref[...])
            for o in range(2):
                here = spec_ref[o, 0, e].astype(F32)
                if e == 0:
                    below = below_ref[o, 0, 0].astype(F32) * has_below
                else:
                    below = spec_ref[o, 0, e - 1].astype(F32)
                if e == BE - 1:
                    above = above_ref[o, 0, 0].astype(F32) * has_above
                else:
                    above = spec_ref[o, 0, e + 1].astype(F32)
                kinetic = planar_ref[...] * here + 0.5 * (2.0 * here - above - below)
                out_ref[o, 0, e] = (result[:, o * Y : (o + 1) * Y] + kinetic).astype(BF16)


def to_waves(grid, orbitals):
    cx, sx = cos_sin(X)
    x = np.arange(X).reshape(PAIRS, 2, BE // 2, 2)
    tables = []
    for low in range(2):
        own = x[..., low].reshape(PAIRS, 8)
        re, im = np.zeros((2 * X, PAIRS, 8)), np.zeros((2 * X, PAIRS, 8))
        re[:X], re[X:] = cx[:, own], -sx[:, own]
        im[:X], im[X:] = sx[:, own], cx[:, own]
        tables.append(np.stack([re, im], axis=2).reshape(2 * X, X))
    tx = bf16_table(np.stack(tables))
    spot = np.arange(256).reshape(2, 2, BE, BE).transpose(1, 2, 0, 3).reshape(-1)
    unit = bf16_table(np.eye(256)[spot])
    cy, sy = cos_sin(Y)
    ty = bf16_table(np.block([[cy, -sy], [sy, cy]]))
    wave_x = np.minimum(np.arange(X), X - np.arange(X)).astype(np.float32) / X
    wave_y = np.minimum(np.arange(Y), Y - np.arange(Y)).astype(np.float32) / Y
    planar = jnp.asarray(
        KINETIC_SCALE * (wave_x[:, None] * wave_x[:, None] + wave_y[None, :] * wave_y[None, :]), dtype=F32
    )
    return pl.pallas_call(
        to_waves_kernel,
        grid=(NSLAB,),
        in_specs=[
            pl.BlockSpec((NBAND, 1, X, 128), lambda s: (0, s, 0, 0)),
            pl.BlockSpec((2, 1, BE, X, Y), lambda s: (0, 0, s, 0, 0)),
            pl.BlockSpec((2, 1, 1, X, Y), lambda s: (0, 0, jnp.maximum(s * BE - 1, 0), 0, 0)),
            pl.BlockSpec((2, 1, 1, X, Y), lambda s: (0, 0, jnp.minimum(s * BE + BE, NZ - 1), 0, 0)),
            pl.BlockSpec((256, 256), lambda s: (0, 0)),
            pl.BlockSpec((2, 2 * X, X), lambda s: (0, 0, 0)),
            pl.BlockSpec((2 * Y, 2 * Y), lambda s: (0, 0)),
            pl.BlockSpec((X, Y), lambda s: (0, 0)),
        ],
        out_specs=pl.BlockSpec((2, 1, BE, X, Y), lambda s: (0, 0, s, 0, 0)),
        out_shape=jax.ShapeDtypeStruct((2, 1, NZ, X, Y), BF16),
        scratch_shapes=[pltpu.VMEM((2, BE, NBAND, BE, X), F32)],
        compiler_params=pltpu.CompilerParams(vmem_limit_bytes=VMEM_LIMIT),
        name="to_waves",
    )(grid, orbitals, orbitals, orbitals, unit, tx, ty, planar)


def exchange(array):
    return lax.all_to_all(array, AXES, split_axis=0, concat_axis=0, tiled=True)


def on_device(orbitals, potential, projector, block_group, strengths):
    groups = block_group.reshape(-1)
    order = point_order()
    turn = np.zeros((P_SIZE, P_SIZE), np.float32)
    turn[order, np.arange(P_SIZE)] = 1.0
    proj = nn(projector.reshape(XB * KB * C, P_SIZE), jnp.asarray(turn, dtype=BF16)).astype(BF16)
    proj = proj.reshape(XB, KB * C, P_SIZE)
    pot = potential.reshape(XB, BE, BE, BE).transpose(0, 2, 1, 3).reshape(XB, 1, P_SIZE)
    own = lax.axis_index(AXES)
    strength = lax.dynamic_slice_in_dim(strengths, own, 1, 0)

    bricks = exchange(to_grid(orbitals).reshape(NDEV, X, 128))
    sums = project(groups, bricks, proj)
    coupled = exchange(couple(exchange(sums.reshape(NDEV, PROJ, ROWS)), strength))
    acted = act(groups, coupled.reshape(NGROUP, C, ROWS), bricks, proj, pot)
    returned = exchange(acted).reshape(NBAND, NSLAB, X, 128)
    return to_waves(returned, orbitals)


def solution(mesh):
    in_specs = (
        P(None, AXES, None, None, None),
        P("slab", None, "band", None),
        P("slab", None, "band", None, None, None),
        P("slab", None, "band", None),
        P(),
    )
    out_specs = P(None, AXES, None, None, None)
    return jax.shard_map(
        on_device, mesh=mesh, in_specs=in_specs, out_specs=out_specs, check_vma=False
    )
```

```python
import math
from itertools import zip_longest

import jax
import jax.numpy as jnp
import numpy as np
from jax import lax
from jax.experimental import pallas as pl
from jax.experimental.pallas import tpu as pltpu
from jax.sharding import PartitionSpec as P

X = 240
Y = 128
NZ = 64
BE = 8
HX = X // 2
P_SIZE = 512
KB = 4
C = 64
PROJ = 8
XB = X // BE
PAIRS = XB // 2
NBAND = 16
NSLAB = 8
NDEV = NBAND * NSLAB
NGROUP = 16
ROWS = 2 * NDEV
HALF = 64
STEP = 3
PROJECT_STEP = 5
PLANES = 4
KINETIC_SCALE = 8.0
AXES = ("band", "slab")
ORDER = ("slab", "band")
F32 = jnp.float32
BF16 = jnp.bfloat16
MIB = 1024 * 1024


def cos_sin(length):
    counter = np.arange(length)
    phases = (counter[:, None] * counter[None, :] % length) * (2.0 * math.pi / length)
    return np.cos(phases) / math.sqrt(length), np.sin(phases) / math.sqrt(length)


def bf16_table(values):
    return jnp.asarray(np.asarray(values, np.float32), dtype=BF16)


def x_order():
    x = np.arange(X).reshape(XB, BE // 2, 2)
    return x.transpose(2, 0, 1).reshape(-1)


def point_order():
    q = np.arange(P_SIZE).reshape(BE, BE, BE)
    return q.transpose(1, 0, 2).reshape(-1)


def nt(a, b):
    return lax.dot_general(a, b, (((1,), (1,)), ((), ())), preferred_element_type=F32)


def nn(a, b):
    return lax.dot_general(a, b, (((1,), (0,)), ((), ())), preferred_element_type=F32)


def two_stages(t, first, second, slots):
    def beside(now, before):
        one = first(now) if now is not None else ()
        two = second(before) if before is not None else ()
        for _ in zip_longest(one, two):
            pass

    pl.when(t == 0)(lambda: beside(slots[0], None))
    pl.when((t > 0) & (t < NSLAB) & (t % 2 == 0))(lambda: beside(slots[0], slots[1]))
    pl.when((t < NSLAB) & (t % 2 == 1))(lambda: beside(slots[1], slots[0]))
    pl.when(t == NSLAB)(lambda: beside(None, slots[(NSLAB - 1) % 2]))


def ahead(t):
    return jnp.minimum(t, NSLAB - 1)


def behind(t):
    return jnp.maximum(t - 1, 0)


def to_grid_kernel(spec_ref, ty_ref, tx_ref, out_ref, *slots):
    def along_y(across_ref):
        for e in range(0, BE, 2):
            across = []
            for i in range(2):
                plane = jnp.concatenate([spec_ref[0, 0, e + i], spec_ref[1, 0, e + i]], axis=1)
                across.append(nt(ty_ref[...], plane))
                if i == 0:
                    yield
            across = jnp.stack([a.reshape(2, NBAND, BE, X) for a in across], axis=2)
            across_ref[:, :, e // 2] = across.reshape(2, NBAND, 2 * BE, X).astype(BF16)
            yield

    def along_x(across_ref):
        low = lax.broadcasted_iota(jnp.int32, (X // 2, 128), 1) < HALF
        for c in range(0, NBAND, 2):
            re = [across_ref[0, c + i].reshape(BE * BE, X) for i in range(2)]
            im = [across_ref[1, c + i].reshape(BE * BE, X) for i in range(2)]
            whole = nt(tx_ref[0], jnp.concatenate([re[0], im[0], re[1], im[1]], axis=0)) + nt(
                tx_ref[1], jnp.concatenate([-im[0], re[0], -im[1], re[1]], axis=0)
            )
            for i in range(2):
                even = whole[: X // 2, i * 128 : (i + 1) * 128]
                odd = whole[X // 2 :, i * 128 : (i + 1) * 128]
                first = jnp.where(low, even, pltpu.roll(odd, HALF, 1))
                second = jnp.where(low, pltpu.roll(even, HALF, 1), odd)
                rows = jnp.stack(
                    [first.reshape(PAIRS, 8, 128), second.reshape(PAIRS, 8, 128)], axis=1
                ).reshape(X, 128)
                out_ref[0, c + i] = rows.astype(BF16)
            yield

    two_stages(pl.program_id(0), along_y, along_x, slots)


def to_grid(orbitals):
    cy, sy = cos_sin(Y)
    ty = bf16_table(np.block([[cy, -sy], [sy, cy]]))
    cx, sx = cos_sin(X)
    order = x_order()
    tx = bf16_table(np.stack([cx[order], sx[order]]))
    return pl.pallas_call(
        to_grid_kernel,
        grid=(NSLAB + 1,),
        in_specs=[
            pl.BlockSpec((2, 1, BE, X, Y), lambda t: (0, 0, ahead(t), 0, 0)),
            pl.BlockSpec((2 * Y, 2 * Y), lambda t: (0, 0)),
            pl.BlockSpec((2, X, X), lambda t: (0, 0, 0)),
        ],
        out_specs=pl.BlockSpec((1, NBAND, X, 128), lambda t: (behind(t), 0, 0, 0)),
        out_shape=jax.ShapeDtypeStruct((NSLAB, NBAND, X, 128), BF16),
        scratch_shapes=[pltpu.VMEM((2, NBAND, BE // 2, 2 * BE, X), BF16)] * 2,
        compiler_params=pltpu.CompilerParams(vmem_limit_bytes=60 * MIB),
        name="to_grid",
    )(orbitals, ty, tx)


def turned_rows(bricks_ref, pair):
    turned = jnp.swapaxes(bricks_ref[:, pair * 16 : (pair + 1) * 16], 0, 1)
    return [
        jnp.concatenate(
            [
                jnp.concatenate([turned[part * 8 + low * 4 + high] for high in range(4)], axis=1)
                for part in range(2)
            ],
            axis=0,
        )
        for low in range(2)
    ]


def project_kernel(groups_ref, bricks_ref, proj_ref, sums_ref, coef_ref):
    t = pl.program_id(0)

    @pl.when(t == 0)
    def _():
        coef_ref[...] = jnp.zeros_like(coef_ref)

    for pair in range(PROJECT_STEP):
        rows = turned_rows(bricks_ref, pair)
        for low in range(2):
            b = 2 * pair + low
            partial = nt(proj_ref[b], rows[low])
            for k in range(KB):
                g = groups_ref[(2 * PROJECT_STEP * t + b) * KB + k]
                coef_ref[g] += partial[k * C : (k + 1) * C]

    @pl.when(t == PAIRS // PROJECT_STEP - 1)
    def _():
        sums_ref[...] = coef_ref[...].astype(BF16)


def project(groups, bricks, proj):
    return pl.pallas_call(
        project_kernel,
        grid_spec=pltpu.PrefetchScalarGridSpec(
            num_scalar_prefetch=1,
            grid=(PAIRS // PROJECT_STEP,),
            in_specs=[
                pl.BlockSpec((NDEV, 16 * PROJECT_STEP, 128), lambda t, g: (0, t, 0)),
                pl.BlockSpec((2 * PROJECT_STEP, KB * C, P_SIZE), lambda t, g: (t, 0, 0)),
            ],
            out_specs=pl.BlockSpec((NGROUP, C, ROWS), lambda t, g: (0, 0, 0)),
            scratch_shapes=[pltpu.VMEM((NGROUP, C, ROWS), F32)],
        ),
        out_shape=jax.ShapeDtypeStruct((NGROUP, C, ROWS), BF16),
        compiler_params=pltpu.CompilerParams(vmem_limit_bytes=60 * MIB),
        name="project",
    )(groups, bricks, proj)


def couple_kernel(sums_ref, strength_ref, out_ref):
    total = jnp.sum(sums_ref[...].astype(F32), axis=0)
    strength = 0.5 * (strength_ref[0] + strength_ref[0].T)
    scaled = strength[:, 0:1] * total[0:1]
    for j in range(1, PROJ):
        scaled = scaled + strength[:, j : j + 1] * total[j : j + 1]
    out_ref[...] = jnp.broadcast_to(scaled[None], (NDEV, PROJ, ROWS)).astype(BF16)


def couple(sums, strengths):
    return pl.pallas_call(
        couple_kernel,
        out_shape=jax.ShapeDtypeStruct((NDEV, PROJ, ROWS), BF16),
        compiler_params=pltpu.CompilerParams(vmem_limit_bytes=8 * MIB),
        name="couple",
    )(sums, strengths)


def act_kernel(groups_ref, coupled_ref, bricks_ref, proj_ref, pot_ref, out_ref, picks_ref):
    t = pl.program_id(0)

    @pl.when(t == 0)
    def _():
        unit = (
            lax.broadcasted_iota(jnp.int32, (ROWS, ROWS), 0)
            == lax.broadcasted_iota(jnp.int32, (ROWS, ROWS), 1)
        ).astype(BF16)
        zeros = jnp.zeros((C, ROWS), BF16)
        for g in range(NGROUP):
            block = coupled_ref[g]
            both = nt(unit, jnp.concatenate([block, zeros, zeros, block], axis=0)).astype(BF16)
            picks_ref[0, g] = both[:, : 2 * C]
            picks_ref[1, g] = both[:, 2 * C :]

    for pair in range(STEP):
        rows = turned_rows(bricks_ref, pair)
        pieces = [None] * 16
        for low in range(2):
            b = 2 * pair + low
            g = [groups_ref[(2 * STEP * t + b) * KB + k] for k in range(KB)]
            picked = jnp.concatenate(
                [picks_ref[0, g[0]] + picks_ref[1, g[1]], picks_ref[0, g[2]] + picks_ref[1, g[3]]],
                axis=1,
            )
            acted = nn(picked, proj_ref[b]) + pot_ref[b] * rows[low].astype(F32)
            acted = acted.astype(BF16)
            for part in range(2):
                for high in range(4):
                    pieces[part * 8 + low * 4 + high] = acted[
                        part * NDEV : (part + 1) * NDEV, high * 128 : (high + 1) * 128
                    ]
        out_ref[:, pair * 16 : (pair + 1) * 16] = jnp.swapaxes(jnp.stack(pieces), 0, 1)


def act(groups, coupled, bricks, proj, pot):
    return pl.pallas_call(
        act_kernel,
        grid_spec=pltpu.PrefetchScalarGridSpec(
            num_scalar_prefetch=1,
            grid=(PAIRS // STEP,),
            in_specs=[
                pl.BlockSpec((NGROUP, C, ROWS), lambda t, g: (0, 0, 0)),
                pl.BlockSpec((NDEV, 16 * STEP, 128), lambda t, g: (0, t, 0)),
                pl.BlockSpec((2 * STEP, KB * C, P_SIZE), lambda t, g: (t, 0, 0)),
                pl.BlockSpec((2 * STEP, 1, P_SIZE), lambda t, g: (t, 0, 0)),
            ],
            out_specs=pl.BlockSpec((NDEV, 16 * STEP, 128), lambda t, g: (0, t, 0)),
            scratch_shapes=[pltpu.VMEM((2, NGROUP, ROWS, 2 * C), BF16)],
        ),
        out_shape=pltpu.VMEM((NDEV, X, 128), BF16),
        compiler_params=pltpu.CompilerParams(vmem_limit_bytes=48 * MIB),
        name="act",
    )(groups, coupled, bricks, proj, pot)


def to_waves_kernel(
    grid_ref, spec_ref, below_ref, above_ref, tx_ref, ty_ref, planar_ref, out_ref, *slots
):
    t = pl.program_id(0)
    has_below = (t > 1).astype(F32)
    has_above = (t < NSLAB).astype(F32)

    def turn(turned_ref):
        for c in range(0, NBAND, 2):
            turned = [grid_ref[0, c + i].T.astype(F32).reshape(2, BE, 1, BE, X) for i in range(2)]
            turned = jnp.concatenate(turned, axis=2).reshape(2, BE, 2 * BE, X)
            turned_ref[:, :, c // 2] = turned.astype(BF16)
            yield

    def apply(turned_ref):
        for first in range(0, BE, PLANES):
            even = turned_ref[0, first : first + PLANES].reshape(PLANES * Y, X)
            odd = turned_ref[1, first : first + PLANES].reshape(PLANES * Y, X)
            even, odd = nt(tx_ref[0], even), nt(tx_ref[1], odd)
            front, back = even + odd, even - odd
            for i in range(PLANES):
                e = first + i
                cols = slice(i * Y, (i + 1) * Y)
                half = [
                    jnp.concatenate([front[o * HX : (o + 1) * HX, cols], back[o * HX : (o + 1) * HX, cols]], axis=0)
                    for o in range(2)
                ]
                half = jnp.concatenate(half, axis=1).astype(BF16)
                result = nn(half, ty_ref[...])
                for o in range(2):
                    here = spec_ref[o, 0, e].astype(F32)
                    if e == 0:
                        below = below_ref[o, 0, 0].astype(F32) * has_below
                    else:
                        below = spec_ref[o, 0, e - 1].astype(F32)
                    if e == BE - 1:
                        above = above_ref[o, 0, 0].astype(F32) * has_above
                    else:
                        above = spec_ref[o, 0, e + 1].astype(F32)
                    kinetic = planar_ref[...] * here - 0.5 * (above + below)
                    out_ref[o, 0, e] = (result[:, o * Y : (o + 1) * Y] + kinetic).astype(BF16)
                yield

    two_stages(t, turn, apply, slots)


def to_waves(grid, orbitals):
    cx, sx = cos_sin(X)
    x = np.arange(X).reshape(PAIRS, 2, BE // 2, 2)
    tables = []
    for low in range(2):
        own = x[..., low].reshape(PAIRS, 8)
        cos, sin = cx[:HX, own], sx[:HX, own]
        re, im = np.concatenate([cos, -sin]), np.concatenate([sin, cos])
        tables.append(np.stack([re, im], axis=2).reshape(X, X))
    tx = bf16_table(np.stack(tables))
    cy, sy = cos_sin(Y)
    ty = bf16_table(np.block([[cy, -sy], [sy, cy]]))
    wave_x = np.minimum(np.arange(X), X - np.arange(X)).astype(np.float32) / X
    wave_y = np.minimum(np.arange(Y), Y - np.arange(Y)).astype(np.float32) / Y
    planar = jnp.asarray(
        KINETIC_SCALE * (wave_x[:, None] * wave_x[:, None] + wave_y[None, :] * wave_y[None, :]) + 1.0, dtype=F32
    )
    return pl.pallas_call(
        to_waves_kernel,
        grid=(NSLAB + 1,),
        in_specs=[
            pl.BlockSpec((1, NBAND, X, 128), lambda t: (ahead(t), 0, 0, 0)),
            pl.BlockSpec((2, 1, BE, X, Y), lambda t: (0, 0, behind(t), 0, 0)),
            pl.BlockSpec((2, 1, 1, X, Y), lambda t: (0, 0, jnp.maximum(behind(t) * BE - 1, 0), 0, 0)),
            pl.BlockSpec((2, 1, 1, X, Y), lambda t: (0, 0, jnp.minimum(behind(t) * BE + BE, NZ - 1), 0, 0)),
            pl.BlockSpec((2, X, X), lambda t: (0, 0, 0)),
            pl.BlockSpec((2 * Y, 2 * Y), lambda t: (0, 0)),
            pl.BlockSpec((X, Y), lambda t: (0, 0)),
        ],
        out_specs=pl.BlockSpec((2, 1, BE, X, Y), lambda t: (0, 0, behind(t), 0, 0)),
        out_shape=jax.ShapeDtypeStruct((2, 1, NZ, X, Y), BF16),
        scratch_shapes=[pltpu.VMEM((2, BE, NBAND // 2, 2 * BE, X), BF16)] * 2,
        compiler_params=pltpu.CompilerParams(vmem_limit_bytes=48 * MIB),
        name="to_waves",
    )(grid, orbitals, orbitals, orbitals, tx, ty, planar)


def exchange(array):
    return lax.all_to_all(array, ORDER, split_axis=0, concat_axis=0, tiled=True)


def on_device(orbitals, potential, projector, block_group, strengths):
    groups = block_group.reshape(-1)
    order = point_order()
    turn = np.zeros((P_SIZE, P_SIZE), np.float32)
    turn[order, np.arange(P_SIZE)] = 1.0
    proj = nn(projector.reshape(XB * KB * C, P_SIZE), jnp.asarray(turn, dtype=BF16)).astype(BF16)
    proj = proj.reshape(XB, KB * C, P_SIZE)
    pot = potential.reshape(XB, BE, BE, BE).transpose(0, 2, 1, 3).reshape(XB, 1, P_SIZE)
    own = lax.axis_index(ORDER)
    strength = lax.dynamic_slice_in_dim(strengths, own, 1, 0)

    bricks = exchange(to_grid(orbitals).reshape(NDEV, X, 128))
    sums = project(groups, bricks, proj)
    coupled = exchange(couple(exchange(sums.reshape(NDEV, PROJ, ROWS)), strength))
    acted = act(groups, coupled.reshape(NGROUP, C, ROWS), bricks, proj, pot)
    returned = exchange(acted).reshape(NSLAB, NBAND, X, 128)
    return to_waves(returned, orbitals)


def solution(mesh):
    in_specs = (
        P(None, AXES, None, None, None),
        P("slab", None, "band", None),
        P("slab", None, "band", None, None, None),
        P("slab", None, "band", None),
        P(),
    )
    out_specs = P(None, AXES, None, None, None)
    return jax.shard_map(
        on_device, mesh=mesh, in_specs=in_specs, out_specs=out_specs, check_vma=False
    )
```

```python
import math
from itertools import zip_longest

import jax
import jax.numpy as jnp
import numpy as np
from jax import lax
from jax.experimental import pallas as pl
from jax.experimental.pallas import tpu as pltpu
from jax.sharding import PartitionSpec as P

X = 240
Y = 128
NZ = 64
BE = 8
HX = X // 2
P_SIZE = 512
KB = 4
C = 64
PROJ = 8
XB = X // BE
PAIRS = XB // 2
NBAND = 16
NSLAB = 8
NDEV = NBAND * NSLAB
NGROUP = 16
ROWS = 2 * NDEV
HALF = 64
STEP = 3
PROJECT_STEP = 5
PLANES = 4
KINETIC_SCALE = 8.0
AXES = ("band", "slab")
ORDER = ("slab", "band")
F32 = jnp.float32
BF16 = jnp.bfloat16
MIB = 1024 * 1024


def cos_sin(length):
    counter = np.arange(length)
    phases = (counter[:, None] * counter[None, :] % length) * (2.0 * math.pi / length)
    return np.cos(phases) / math.sqrt(length), np.sin(phases) / math.sqrt(length)


def bf16_table(values):
    return jnp.asarray(np.asarray(values, np.float32), dtype=BF16)


def x_order():
    x = np.arange(X).reshape(XB, BE // 2, 2)
    return x.transpose(2, 0, 1).reshape(-1)


def point_order():
    q = np.arange(P_SIZE).reshape(BE, BE, BE)
    return q.transpose(1, 0, 2).reshape(-1)


def nt(a, b):
    return lax.dot_general(a, b, (((1,), (1,)), ((), ())), preferred_element_type=F32)


def nn(a, b):
    return lax.dot_general(a, b, (((1,), (0,)), ((), ())), preferred_element_type=F32)


def two_stages(t, first, second, slots):
    def beside(now, before):
        one = first(now) if now is not None else ()
        two = second(before) if before is not None else ()
        for _ in zip_longest(one, two):
            pass

    pl.when(t == 0)(lambda: beside(slots[0], None))
    pl.when((t > 0) & (t < NSLAB) & (t % 2 == 0))(lambda: beside(slots[0], slots[1]))
    pl.when((t < NSLAB) & (t % 2 == 1))(lambda: beside(slots[1], slots[0]))
    pl.when(t == NSLAB)(lambda: beside(None, slots[(NSLAB - 1) % 2]))


def ahead(t):
    return jnp.minimum(t, NSLAB - 1)


def behind(t):
    return jnp.maximum(t - 1, 0)


def to_grid_kernel(spec_ref, ty_ref, tx_ref, out_ref, *slots):
    def along_y(across_ref):
        for e in range(0, BE, 2):
            across = []
            for i in range(2):
                plane = jnp.concatenate([spec_ref[0, 0, e + i], spec_ref[1, 0, e + i]], axis=1)
                across.append(nt(ty_ref[...], plane))
                if i == 0:
                    yield
            across = jnp.stack([a.reshape(2, NBAND, BE, X) for a in across], axis=2)
            across_ref[:, :, e // 2] = across.reshape(2, NBAND, 2 * BE, X).astype(BF16)
            yield

    def along_x(across_ref):
        low = lax.broadcasted_iota(jnp.int32, (X // 2, 128), 1) < HALF
        for c in range(0, NBAND, 2):
            re = [across_ref[0, c + i].reshape(BE * BE, X) for i in range(2)]
            im = [across_ref[1, c + i].reshape(BE * BE, X) for i in range(2)]
            whole = nt(tx_ref[0], jnp.concatenate([re[0], im[0], re[1], im[1]], axis=0)) + nt(
                tx_ref[1], jnp.concatenate([-im[0], re[0], -im[1], re[1]], axis=0)
            )
            for i in range(2):
                even = whole[: X // 2, i * 128 : (i + 1) * 128]
                odd = whole[X // 2 :, i * 128 : (i + 1) * 128]
                first = jnp.where(low, even, pltpu.roll(odd, HALF, 1))
                second = jnp.where(low, pltpu.roll(even, HALF, 1), odd)
                rows = jnp.stack(
                    [first.reshape(PAIRS, 8, 128), second.reshape(PAIRS, 8, 128)], axis=1
                ).reshape(X, 128)
                out_ref[0, c + i] = rows.astype(BF16)
            yield

    two_stages(pl.program_id(0), along_y, along_x, slots)


def to_grid(orbitals):
    cy, sy = cos_sin(Y)
    ty = bf16_table(np.block([[cy, -sy], [sy, cy]]))
    cx, sx = cos_sin(X)
    order = x_order()
    tx = bf16_table(np.stack([cx[order], sx[order]]))
    return pl.pallas_call(
        to_grid_kernel,
        grid=(NSLAB + 1,),
        in_specs=[
            pl.BlockSpec((2, 1, BE, X, Y), lambda t: (0, 0, ahead(t), 0, 0)),
            pl.BlockSpec((2 * Y, 2 * Y), lambda t: (0, 0)),
            pl.BlockSpec((2, X, X), lambda t: (0, 0, 0)),
        ],
        out_specs=pl.BlockSpec((1, NBAND, X, 128), lambda t: (behind(t), 0, 0, 0)),
        out_shape=pltpu.VMEM((NSLAB, NBAND, X, 128), BF16),
        scratch_shapes=[pltpu.VMEM((2, NBAND, BE // 2, 2 * BE, X), BF16)] * 2,
        compiler_params=pltpu.CompilerParams(vmem_limit_bytes=52 * MIB),
        name="to_grid",
    )(orbitals, ty, tx)


def turned_rows(bricks_ref, pair):
    turned = jnp.swapaxes(bricks_ref[:, pair * 16 : (pair + 1) * 16], 0, 1)
    return [
        jnp.concatenate(
            [
                jnp.concatenate([turned[part * 8 + low * 4 + high] for high in range(4)], axis=1)
                for part in range(2)
            ],
            axis=0,
        )
        for low in range(2)
    ]


def project_kernel(groups_ref, bricks_ref, natural_ref, turn_ref, proj_ref, sums_ref, coef_ref):
    t = pl.program_id(0)

    @pl.when(t == 0)
    def _():
        coef_ref[...] = jnp.zeros_like(coef_ref)

    for pair in range(PROJECT_STEP):
        rows = turned_rows(bricks_ref, pair)
        for low in range(2):
            b = 2 * pair + low
            proj_ref[b] = nn(natural_ref[b], turn_ref[...]).astype(BF16)
            partial = nt(proj_ref[b], rows[low])
            for k in range(KB):
                g = groups_ref[(2 * PROJECT_STEP * t + b) * KB + k]
                coef_ref[g] += partial[k * C : (k + 1) * C]

    @pl.when(t == PAIRS // PROJECT_STEP - 1)
    def _():
        sums_ref[...] = coef_ref[...].astype(BF16)


def project(groups, bricks, natural):
    turn = np.zeros((P_SIZE, P_SIZE))
    turn[point_order(), np.arange(P_SIZE)] = 1.0
    return pl.pallas_call(
        project_kernel,
        grid_spec=pltpu.PrefetchScalarGridSpec(
            num_scalar_prefetch=1,
            grid=(PAIRS // PROJECT_STEP,),
            in_specs=[
                pl.BlockSpec((NDEV, 16 * PROJECT_STEP, 128), lambda t, g: (0, t, 0)),
                pl.BlockSpec((2 * PROJECT_STEP, KB * C, P_SIZE), lambda t, g: (t, 0, 0)),
                pl.BlockSpec((P_SIZE, P_SIZE), lambda t, g: (0, 0)),
            ],
            out_specs=[
                pl.BlockSpec((2 * PROJECT_STEP, KB * C, P_SIZE), lambda t, g: (t, 0, 0)),
                pl.BlockSpec((NGROUP, C, ROWS), lambda t, g: (0, 0, 0)),
            ],
            scratch_shapes=[pltpu.VMEM((NGROUP, C, ROWS), F32)],
        ),
        out_shape=[
            jax.ShapeDtypeStruct((XB, KB * C, P_SIZE), BF16),
            jax.ShapeDtypeStruct((NGROUP, C, ROWS), BF16),
        ],
        compiler_params=pltpu.CompilerParams(vmem_limit_bytes=50 * MIB),
        name="project",
    )(groups, bricks, natural, bf16_table(turn))


def couple_kernel(sums_ref, strength_ref, out_ref):
    total = jnp.sum(sums_ref[...].astype(F32), axis=0)
    strength = 0.5 * (strength_ref[0] + strength_ref[0].T)
    scaled = strength[:, 0:1] * total[0:1]
    for j in range(1, PROJ):
        scaled = scaled + strength[:, j : j + 1] * total[j : j + 1]
    out_ref[...] = jnp.broadcast_to(scaled[None], (NDEV, PROJ, ROWS)).astype(BF16)


def couple(sums, strengths):
    return pl.pallas_call(
        couple_kernel,
        out_shape=jax.ShapeDtypeStruct((NDEV, PROJ, ROWS), BF16),
        compiler_params=pltpu.CompilerParams(vmem_limit_bytes=8 * MIB),
        name="couple",
    )(sums, strengths)


def act_kernel(groups_ref, coupled_ref, bricks_ref, proj_ref, pot_ref, out_ref, picks_ref):
    t = pl.program_id(0)

    @pl.when(t == 0)
    def _():
        unit = (
            lax.broadcasted_iota(jnp.int32, (ROWS, ROWS), 0)
            == lax.broadcasted_iota(jnp.int32, (ROWS, ROWS), 1)
        ).astype(BF16)
        zeros = jnp.zeros((C, ROWS), BF16)
        for g in range(NGROUP):
            block = coupled_ref[g]
            both = nt(unit, jnp.concatenate([block, zeros, zeros, block], axis=0)).astype(BF16)
            picks_ref[0, g] = both[:, : 2 * C]
            picks_ref[1, g] = both[:, 2 * C :]

    for pair in range(STEP):
        rows = turned_rows(bricks_ref, pair)
        pieces = [None] * 16
        for low in range(2):
            b = 2 * pair + low
            g = [groups_ref[(2 * STEP * t + b) * KB + k] for k in range(KB)]
            picked = jnp.concatenate(
                [picks_ref[0, g[0]] + picks_ref[1, g[1]], picks_ref[0, g[2]] + picks_ref[1, g[3]]],
                axis=1,
            )
            acted = nn(picked, proj_ref[b]) + pot_ref[b] * rows[low].astype(F32)
            acted = acted.astype(BF16)
            for part in range(2):
                for high in range(4):
                    pieces[part * 8 + low * 4 + high] = acted[
                        part * NDEV : (part + 1) * NDEV, high * 128 : (high + 1) * 128
                    ]
        out_ref[:, pair * 16 : (pair + 1) * 16] = jnp.swapaxes(jnp.stack(pieces), 0, 1)


def act(groups, coupled, bricks, proj, pot):
    return pl.pallas_call(
        act_kernel,
        grid_spec=pltpu.PrefetchScalarGridSpec(
            num_scalar_prefetch=1,
            grid=(PAIRS // STEP,),
            in_specs=[
                pl.BlockSpec((NGROUP, C, ROWS), lambda t, g: (0, 0, 0)),
                pl.BlockSpec((NDEV, 16 * STEP, 128), lambda t, g: (0, t, 0)),
                pl.BlockSpec((2 * STEP, KB * C, P_SIZE), lambda t, g: (t, 0, 0)),
                pl.BlockSpec((2 * STEP, 1, P_SIZE), lambda t, g: (t, 0, 0)),
            ],
            out_specs=pl.BlockSpec((NDEV, 16 * STEP, 128), lambda t, g: (0, t, 0)),
            scratch_shapes=[pltpu.VMEM((2, NGROUP, ROWS, 2 * C), BF16)],
        ),
        out_shape=pltpu.VMEM((NDEV, X, 128), BF16),
        compiler_params=pltpu.CompilerParams(vmem_limit_bytes=48 * MIB),
        name="act",
    )(groups, coupled, bricks, proj, pot)


def to_waves_kernel(
    grid_ref, spec_ref, below_ref, above_ref, tx_ref, ty_ref, planar_ref, out_ref, *slots
):
    t = pl.program_id(0)
    has_below = (t > 1).astype(F32)
    has_above = (t < NSLAB).astype(F32)

    def turn(turned_ref):
        for c in range(0, NBAND, 2):
            turned = [grid_ref[0, c + i].T.astype(F32).reshape(2, BE, 1, BE, X) for i in range(2)]
            turned = jnp.concatenate(turned, axis=2).reshape(2, BE, 2 * BE, X)
            turned_ref[:, :, c // 2] = turned.astype(BF16)
            yield

    def apply(turned_ref):
        for first in range(0, BE, PLANES):
            even = turned_ref[0, first : first + PLANES].reshape(PLANES * Y, X)
            odd = turned_ref[1, first : first + PLANES].reshape(PLANES * Y, X)
            even, odd = nt(tx_ref[0], even), nt(tx_ref[1], odd)
            front, back = even + odd, even - odd
            for i in range(PLANES):
                e = first + i
                cols = slice(i * Y, (i + 1) * Y)
                half = [
                    jnp.concatenate([front[o * HX : (o + 1) * HX, cols], back[o * HX : (o + 1) * HX, cols]], axis=0)
                    for o in range(2)
                ]
                half = jnp.concatenate(half, axis=1).astype(BF16)
                result = nn(half, ty_ref[...])
                for o in range(2):
                    here = spec_ref[o, 0, e].astype(F32)
                    if e == 0:
                        below = below_ref[o, 0, 0].astype(F32) * has_below
                    else:
                        below = spec_ref[o, 0, e - 1].astype(F32)
                    if e == BE - 1:
                        above = above_ref[o, 0, 0].astype(F32) * has_above
                    else:
                        above = spec_ref[o, 0, e + 1].astype(F32)
                    kinetic = planar_ref[...] * here - 0.5 * (above + below)
                    out_ref[o, 0, e] = (result[:, o * Y : (o + 1) * Y] + kinetic).astype(BF16)
                yield

    two_stages(t, turn, apply, slots)


def to_waves(grid, orbitals):
    cx, sx = cos_sin(X)
    x = np.arange(X).reshape(PAIRS, 2, BE // 2, 2)
    tables = []
    for low in range(2):
        own = x[..., low].reshape(PAIRS, 8)
        cos, sin = cx[:HX, own], sx[:HX, own]
        re, im = np.concatenate([cos, -sin]), np.concatenate([sin, cos])
        tables.append(np.stack([re, im], axis=2).reshape(X, X))
    tx = bf16_table(np.stack(tables))
    cy, sy = cos_sin(Y)
    ty = bf16_table(np.block([[cy, -sy], [sy, cy]]))
    wave_x = np.minimum(np.arange(X), X - np.arange(X)).astype(np.float32) / X
    wave_y = np.minimum(np.arange(Y), Y - np.arange(Y)).astype(np.float32) / Y
    planar = jnp.asarray(
        KINETIC_SCALE * (wave_x[:, None] * wave_x[:, None] + wave_y[None, :] * wave_y[None, :]) + 1.0, dtype=F32
    )
    return pl.pallas_call(
        to_waves_kernel,
        grid=(NSLAB + 1,),
        in_specs=[
            pl.BlockSpec((1, NBAND, X, 128), lambda t: (ahead(t), 0, 0, 0)),
            pl.BlockSpec((2, 1, BE, X, Y), lambda t: (0, 0, behind(t), 0, 0)),
            pl.BlockSpec((2, 1, 1, X, Y), lambda t: (0, 0, jnp.maximum(behind(t) * BE - 1, 0), 0, 0)),
            pl.BlockSpec((2, 1, 1, X, Y), lambda t: (0, 0, jnp.minimum(behind(t) * BE + BE, NZ - 1), 0, 0)),
            pl.BlockSpec((2, X, X), lambda t: (0, 0, 0)),
            pl.BlockSpec((2 * Y, 2 * Y), lambda t: (0, 0)),
            pl.BlockSpec((X, Y), lambda t: (0, 0)),
        ],
        out_specs=pl.BlockSpec((2, 1, BE, X, Y), lambda t: (0, 0, behind(t), 0, 0)),
        out_shape=jax.ShapeDtypeStruct((2, 1, NZ, X, Y), BF16),
        scratch_shapes=[pltpu.VMEM((2, BE, NBAND // 2, 2 * BE, X), BF16)] * 2,
        compiler_params=pltpu.CompilerParams(vmem_limit_bytes=48 * MIB),
        name="to_waves",
    )(grid, orbitals, orbitals, orbitals, tx, ty, planar)


def exchange(array):
    return lax.all_to_all(array, ORDER, split_axis=0, concat_axis=0, tiled=True)


def on_device(orbitals, potential, projector, block_group, strengths):
    groups = block_group.reshape(-1)
    strength = lax.dynamic_slice_in_dim(strengths, lax.axis_index(ORDER), 1, 0)
    grid, groups, strength = lax.optimization_barrier(
        (to_grid(orbitals).reshape(NDEV, X, 128), groups, strength)
    )
    bricks = exchange(grid)
    proj, sums = project(groups, bricks, projector.reshape(XB, KB * C, P_SIZE))
    sums, potential = lax.optimization_barrier((exchange(sums.reshape(NDEV, PROJ, ROWS)), potential))
    pot = potential.reshape(XB, BE, BE, BE).transpose(0, 2, 1, 3).reshape(XB, 1, P_SIZE)
    coupled = exchange(couple(sums, strength)).reshape(NGROUP, C, ROWS)
    coupled = pltpu.with_memory_space_constraint(coupled, pltpu.VMEM)
    acted = act(groups, coupled, bricks, proj, pot)
    returned = exchange(acted).reshape(NSLAB, NBAND, X, 128)
    return to_waves(returned, orbitals)


def solution(mesh):
    in_specs = (
        P(None, AXES, None, None, None),
        P("slab", None, "band", None),
        P("slab", None, "band", None, None, None),
        P("slab", None, "band", None),
        P(),
    )
    out_specs = P(None, AXES, None, None, None)
    return jax.shard_map(
        on_device, mesh=mesh, in_specs=in_specs, out_specs=out_specs, check_vma=False
    )
```

```python
import math
from itertools import zip_longest

import jax
import jax.numpy as jnp
import numpy as np
from jax import lax
from jax.experimental import pallas as pl
from jax.experimental.pallas import tpu as pltpu
from jax.sharding import PartitionSpec as P

X = 240
Y = 128
NZ = 64
BE = 8
HX = X // 2
P_SIZE = 512
KB = 4
C = 64
PROJ = 8
XB = X // BE
PAIRS = XB // 2
NBAND = 16
NSLAB = 8
NDEV = NBAND * NSLAB
NGROUP = 16
ROWS = 2 * NDEV
HALF = 64
STEP = 5
PROJECT_STEP = 5
PLANES = 4
KINETIC_SCALE = 8.0
AXES = ("band", "slab")
ORDER = ("slab", "band")
F32 = jnp.float32
BF16 = jnp.bfloat16
MIB = 1024 * 1024


def cos_sin(length):
    counter = np.arange(length)
    phases = (counter[:, None] * counter[None, :] % length) * (2.0 * math.pi / length)
    return np.cos(phases) / math.sqrt(length), np.sin(phases) / math.sqrt(length)


def bf16_table(values):
    return jnp.asarray(np.asarray(values, np.float32), dtype=BF16)


def x_order():
    x = np.arange(X).reshape(XB, BE // 2, 2)
    return x.transpose(2, 0, 1).reshape(-1)


def point_order():
    q = np.arange(P_SIZE).reshape(BE, BE, BE)
    return q.transpose(1, 0, 2).reshape(-1)


def nt(a, b):
    return lax.dot_general(a, b, (((1,), (1,)), ((), ())), preferred_element_type=F32)


def nn(a, b):
    return lax.dot_general(a, b, (((1,), (0,)), ((), ())), preferred_element_type=F32)


def two_stages(t, first, second, slots):
    def beside(now, before):
        one = first(now) if now is not None else ()
        two = second(before) if before is not None else ()
        for _ in zip_longest(one, two):
            pass

    pl.when(t == 0)(lambda: beside(slots[0], None))
    pl.when((t > 0) & (t < NSLAB) & (t % 2 == 0))(lambda: beside(slots[0], slots[1]))
    pl.when((t < NSLAB) & (t % 2 == 1))(lambda: beside(slots[1], slots[0]))
    pl.when(t == NSLAB)(lambda: beside(None, slots[(NSLAB - 1) % 2]))


def ahead(t):
    return jnp.minimum(t, NSLAB - 1)


def behind(t):
    return jnp.maximum(t - 1, 0)


def to_grid_kernel(spec_ref, ty_ref, tx_ref, out_ref, *slots):
    def along_y(across_ref):
        for e in range(0, BE, 2):
            across = []
            for i in range(2):
                plane = jnp.concatenate([spec_ref[0, 0, e + i], spec_ref[1, 0, e + i]], axis=1)
                across.append(nt(ty_ref[...], plane))
                if i == 0:
                    yield
            across = jnp.stack([a.reshape(2, NBAND, BE, X) for a in across], axis=2)
            across_ref[:, :, e // 2] = across.reshape(2, NBAND, 2 * BE, X).astype(BF16)
            yield

    def along_x(across_ref):
        low = lax.broadcasted_iota(jnp.int32, (X // 2, 128), 1) < HALF
        for c in range(0, NBAND, 2):
            re = [across_ref[0, c + i].reshape(BE * BE, X) for i in range(2)]
            im = [across_ref[1, c + i].reshape(BE * BE, X) for i in range(2)]
            whole = nt(tx_ref[0], jnp.concatenate([re[0], im[0], re[1], im[1]], axis=0)) + nt(
                tx_ref[1], jnp.concatenate([-im[0], re[0], -im[1], re[1]], axis=0)
            )
            for i in range(2):
                even = whole[: X // 2, i * 128 : (i + 1) * 128]
                odd = whole[X // 2 :, i * 128 : (i + 1) * 128]
                first = jnp.where(low, even, pltpu.roll(odd, HALF, 1))
                second = jnp.where(low, pltpu.roll(even, HALF, 1), odd)
                rows = jnp.stack(
                    [first.reshape(PAIRS, 8, 128), second.reshape(PAIRS, 8, 128)], axis=1
                ).reshape(X, 128)
                out_ref[0, c + i] = rows.astype(BF16)
            yield

    two_stages(pl.program_id(0), along_y, along_x, slots)


def to_grid(orbitals):
    cy, sy = cos_sin(Y)
    ty = bf16_table(np.block([[cy, -sy], [sy, cy]]))
    cx, sx = cos_sin(X)
    order = x_order()
    tx = bf16_table(np.stack([cx[order], sx[order]]))
    return pl.pallas_call(
        to_grid_kernel,
        grid=(NSLAB + 1,),
        in_specs=[
            pl.BlockSpec((2, 1, BE, X, Y), lambda t: (0, 0, ahead(t), 0, 0)),
            pl.BlockSpec((2 * Y, 2 * Y), lambda t: (0, 0)),
            pl.BlockSpec((2, X, X), lambda t: (0, 0, 0)),
        ],
        out_specs=pl.BlockSpec((1, NBAND, X, 128), lambda t: (behind(t), 0, 0, 0)),
        out_shape=pltpu.VMEM((NSLAB, NBAND, X, 128), BF16),
        scratch_shapes=[pltpu.VMEM((2, NBAND, BE // 2, 2 * BE, X), BF16)] * 2,
        compiler_params=pltpu.CompilerParams(vmem_limit_bytes=52 * MIB),
        name="to_grid",
    )(orbitals, ty, tx)


def turned_rows(bricks_ref, pair):
    turned = jnp.swapaxes(bricks_ref[:, pair * 16 : (pair + 1) * 16], 0, 1)
    return [
        jnp.concatenate(
            [
                jnp.concatenate([turned[part * 8 + low * 4 + high] for high in range(4)], axis=1)
                for part in range(2)
            ],
            axis=0,
        )
        for low in range(2)
    ]


def project_kernel(groups_ref, bricks_ref, natural_ref, turn_ref, proj_ref, sums_ref, coef_ref):
    t = pl.program_id(0)

    @pl.when(t == 0)
    def _():
        coef_ref[...] = jnp.zeros_like(coef_ref)

    for pair in range(PROJECT_STEP):
        rows = turned_rows(bricks_ref, pair)
        for low in range(2):
            b = 2 * pair + low
            proj_ref[b] = nn(natural_ref[b], turn_ref[...]).astype(BF16)
            partial = nt(proj_ref[b], rows[low])
            for k in range(KB):
                g = groups_ref[(2 * PROJECT_STEP * t + b) * KB + k]
                coef_ref[g] += partial[k * C : (k + 1) * C]

    @pl.when(t == PAIRS // PROJECT_STEP - 1)
    def _():
        sums_ref[...] = coef_ref[...].astype(BF16)


def project(groups, bricks, natural):
    turn = np.zeros((P_SIZE, P_SIZE))
    turn[point_order(), np.arange(P_SIZE)] = 1.0
    return pl.pallas_call(
        project_kernel,
        grid_spec=pltpu.PrefetchScalarGridSpec(
            num_scalar_prefetch=1,
            grid=(PAIRS // PROJECT_STEP,),
            in_specs=[
                pl.BlockSpec((NDEV, 16 * PROJECT_STEP, 128), lambda t, g: (0, t, 0)),
                pl.BlockSpec((2 * PROJECT_STEP, KB * C, P_SIZE), lambda t, g: (t, 0, 0)),
                pl.BlockSpec((P_SIZE, P_SIZE), lambda t, g: (0, 0)),
            ],
            out_specs=[
                pl.BlockSpec((2 * PROJECT_STEP, KB * C, P_SIZE), lambda t, g: (t, 0, 0)),
                pl.BlockSpec((NGROUP, C, ROWS), lambda t, g: (0, 0, 0)),
            ],
            scratch_shapes=[pltpu.VMEM((NGROUP, C, ROWS), F32)],
        ),
        out_shape=[
            jax.ShapeDtypeStruct((XB, KB * C, P_SIZE), BF16),
            jax.ShapeDtypeStruct((NGROUP, C, ROWS), BF16),
        ],
        compiler_params=pltpu.CompilerParams(vmem_limit_bytes=50 * MIB),
        name="project",
    )(groups, bricks, natural, bf16_table(turn))


def couple_kernel(sums_ref, strength_ref, out_ref):
    total = jnp.sum(sums_ref[...].astype(F32), axis=0)
    strength = 0.5 * (strength_ref[0] + strength_ref[0].T)
    scaled = strength[:, 0:1] * total[0:1]
    for j in range(1, PROJ):
        scaled = scaled + strength[:, j : j + 1] * total[j : j + 1]
    out_ref[...] = jnp.broadcast_to(scaled[None], (NDEV, PROJ, ROWS)).astype(BF16)


def couple(sums, strengths):
    return pl.pallas_call(
        couple_kernel,
        out_shape=jax.ShapeDtypeStruct((NDEV, PROJ, ROWS), BF16),
        compiler_params=pltpu.CompilerParams(vmem_limit_bytes=8 * MIB),
        name="couple",
    )(sums, strengths)


def act_kernel(groups_ref, coupled_ref, bricks_ref, proj_ref, pot_ref, out_ref, picks_ref):
    t = pl.program_id(0)

    @pl.when(t == 0)
    def _():
        unit = (
            lax.broadcasted_iota(jnp.int32, (ROWS, ROWS), 0)
            == lax.broadcasted_iota(jnp.int32, (ROWS, ROWS), 1)
        ).astype(BF16)
        zeros = jnp.zeros((C, ROWS), BF16)
        for g in range(NGROUP):
            block = coupled_ref[g]
            both = nt(unit, jnp.concatenate([block, zeros, zeros, block], axis=0)).astype(BF16)
            picks_ref[0, g] = both[:, : 2 * C]
            picks_ref[1, g] = both[:, 2 * C :]

    for pair in range(STEP):
        rows = turned_rows(bricks_ref, pair)
        pieces = [None] * 16
        for low in range(2):
            b = 2 * pair + low
            g = [groups_ref[(2 * STEP * t + b) * KB + k] for k in range(KB)]
            picked = jnp.concatenate(
                [picks_ref[0, g[0]] + picks_ref[1, g[1]], picks_ref[0, g[2]] + picks_ref[1, g[3]]],
                axis=1,
            )
            acted = nn(picked, proj_ref[b]) + pot_ref[b] * rows[low].astype(F32)
            acted = acted.astype(BF16)
            for part in range(2):
                for high in range(4):
                    pieces[part * 8 + low * 4 + high] = acted[
                        part * NDEV : (part + 1) * NDEV, high * 128 : (high + 1) * 128
                    ]
        out_ref[:, pair * 16 : (pair + 1) * 16] = jnp.swapaxes(jnp.stack(pieces), 0, 1)


def act(groups, coupled, bricks, proj, pot):
    return pl.pallas_call(
        act_kernel,
        grid_spec=pltpu.PrefetchScalarGridSpec(
            num_scalar_prefetch=1,
            grid=(PAIRS // STEP,),
            in_specs=[
                pl.BlockSpec((NGROUP, C, ROWS), lambda t, g: (0, 0, 0)),
                pl.BlockSpec((NDEV, 16 * STEP, 128), lambda t, g: (0, t, 0)),
                pl.BlockSpec((2 * STEP, KB * C, P_SIZE), lambda t, g: (t, 0, 0)),
                pl.BlockSpec((2 * STEP, 1, P_SIZE), lambda t, g: (t, 0, 0)),
            ],
            out_specs=pl.BlockSpec((NDEV, 16 * STEP, 128), lambda t, g: (0, t, 0)),
            scratch_shapes=[pltpu.VMEM((2, NGROUP, ROWS, 2 * C), BF16)],
        ),
        out_shape=pltpu.VMEM((NDEV, X, 128), BF16),
        compiler_params=pltpu.CompilerParams(vmem_limit_bytes=48 * MIB),
        name="act",
    )(groups, coupled, bricks, proj, pot)


def to_waves_kernel(
    grid_ref, spec_ref, below_ref, above_ref, tx_ref, ty_ref, planar_ref, out_ref, *slots
):
    t = pl.program_id(0)
    has_below = (t > 1).astype(F32)
    has_above = (t < NSLAB).astype(F32)

    def turn(turned_ref):
        for c in range(0, NBAND, 2):
            turned = [grid_ref[0, c + i].T.astype(F32).reshape(2, BE, 1, BE, X) for i in range(2)]
            turned = jnp.concatenate(turned, axis=2).reshape(2, BE, 2 * BE, X)
            turned_ref[:, :, c // 2] = turned.astype(BF16)
            yield

    def apply(turned_ref):
        for first in range(0, BE, PLANES):
            even = turned_ref[0, first : first + PLANES].reshape(PLANES * Y, X)
            odd = turned_ref[1, first : first + PLANES].reshape(PLANES * Y, X)
            even, odd = nt(tx_ref[0], even), nt(tx_ref[1], odd)
            front, back = even + odd, even - odd
            for i in range(PLANES):
                e = first + i
                cols = slice(i * Y, (i + 1) * Y)
                half = [
                    jnp.concatenate([front[o * HX : (o + 1) * HX, cols], back[o * HX : (o + 1) * HX, cols]], axis=0)
                    for o in range(2)
                ]
                half = jnp.concatenate(half, axis=1).astype(BF16)
                result = nn(half, ty_ref[...])
                for o in range(2):
                    here = spec_ref[o, 0, e].astype(F32)
                    if e == 0:
                        below = below_ref[o, 0, 0].astype(F32) * has_below
                    else:
                        below = spec_ref[o, 0, e - 1].astype(F32)
                    if e == BE - 1:
                        above = above_ref[o, 0, 0].astype(F32) * has_above
                    else:
                        above = spec_ref[o, 0, e + 1].astype(F32)
                    kinetic = planar_ref[...] * here - 0.5 * (above + below)
                    out_ref[o, 0, e] = (result[:, o * Y : (o + 1) * Y] + kinetic).astype(BF16)
                yield

    two_stages(t, turn, apply, slots)


def to_waves(grid, orbitals):
    cx, sx = cos_sin(X)
    x = np.arange(X).reshape(PAIRS, 2, BE // 2, 2)
    tables = []
    for low in range(2):
        own = x[..., low].reshape(PAIRS, 8)
        cos, sin = cx[:HX, own], sx[:HX, own]
        re, im = np.concatenate([cos, -sin]), np.concatenate([sin, cos])
        tables.append(np.stack([re, im], axis=2).reshape(X, X))
    tx = bf16_table(np.stack(tables))
    cy, sy = cos_sin(Y)
    ty = bf16_table(np.block([[cy, -sy], [sy, cy]]))
    wave_x = np.minimum(np.arange(X), X - np.arange(X)).astype(np.float32) / X
    wave_y = np.minimum(np.arange(Y), Y - np.arange(Y)).astype(np.float32) / Y
    planar = jnp.asarray(
        KINETIC_SCALE * (wave_x[:, None] * wave_x[:, None] + wave_y[None, :] * wave_y[None, :]) + 1.0, dtype=F32
    )
    return pl.pallas_call(
        to_waves_kernel,
        grid=(NSLAB + 1,),
        in_specs=[
            pl.BlockSpec((1, NBAND, X, 128), lambda t: (ahead(t), 0, 0, 0)),
            pl.BlockSpec((2, 1, BE, X, Y), lambda t: (0, 0, behind(t), 0, 0)),
            pl.BlockSpec((2, 1, 1, X, Y), lambda t: (0, 0, jnp.maximum(behind(t) * BE - 1, 0), 0, 0)),
            pl.BlockSpec((2, 1, 1, X, Y), lambda t: (0, 0, jnp.minimum(behind(t) * BE + BE, NZ - 1), 0, 0)),
            pl.BlockSpec((2, X, X), lambda t: (0, 0, 0)),
            pl.BlockSpec((2 * Y, 2 * Y), lambda t: (0, 0)),
            pl.BlockSpec((X, Y), lambda t: (0, 0)),
        ],
        out_specs=pl.BlockSpec((2, 1, BE, X, Y), lambda t: (0, 0, behind(t), 0, 0)),
        out_shape=jax.ShapeDtypeStruct((2, 1, NZ, X, Y), BF16),
        scratch_shapes=[pltpu.VMEM((2, BE, NBAND // 2, 2 * BE, X), BF16)] * 2,
        compiler_params=pltpu.CompilerParams(vmem_limit_bytes=52 * MIB),
        name="to_waves",
    )(grid, orbitals, orbitals, orbitals, tx, ty, planar)


def exchange(array):
    return lax.all_to_all(array, ORDER, split_axis=0, concat_axis=0, tiled=True)


def on_device(orbitals, potential, projector, block_group, strengths):
    groups = block_group.reshape(-1)
    strength = lax.dynamic_slice_in_dim(strengths, lax.axis_index(ORDER), 1, 0)
    grid, groups, strength = lax.optimization_barrier(
        (to_grid(orbitals).reshape(NDEV, X, 128), groups, strength)
    )
    bricks = exchange(grid)
    proj, sums = project(groups, bricks, projector.reshape(XB, KB * C, P_SIZE))
    sums, potential = lax.optimization_barrier((exchange(sums.reshape(NDEV, PROJ, ROWS)), potential))
    pot = potential.reshape(XB, BE, BE, BE).transpose(0, 2, 1, 3).reshape(XB, 1, P_SIZE)
    coupled = exchange(couple(sums, strength)).reshape(NGROUP, C, ROWS)
    coupled = pltpu.with_memory_space_constraint(coupled, pltpu.VMEM)
    acted = act(groups, coupled, bricks, proj, pot)
    returned = exchange(acted).reshape(NSLAB, NBAND, X, 128)
    returned = pltpu.with_memory_space_constraint(returned, pltpu.VMEM)
    return to_waves(returned, orbitals)


def solution(mesh):
    in_specs = (
        P(None, AXES, None, None, None),
        P("slab", None, "band", None),
        P("slab", None, "band", None, None, None),
        P("slab", None, "band", None),
        P(),
    )
    out_specs = P(None, AXES, None, None, None)
    return jax.shard_map(
        on_device, mesh=mesh, in_specs=in_specs, out_specs=out_specs, check_vma=False
    )
```

```python
import math
from itertools import zip_longest

import jax
import jax.numpy as jnp
import numpy as np
from jax import lax
from jax.experimental import pallas as pl
from jax.experimental.pallas import tpu as pltpu
from jax.sharding import PartitionSpec as P

X = 240
Y = 128
NZ = 64
BE = 8
HX = X // 2
P_SIZE = 512
KB = 4
C = 64
PROJ = 8
XB = X // BE
PAIRS = XB // 2
NBAND = 16
NSLAB = 8
NDEV = NBAND * NSLAB
NGROUP = 16
ROWS = 2 * NDEV
HALF = 64
STEP = 5
PROJECT_STEP = 5
PLANES = 4
KINETIC_SCALE = 8.0
AXES = ("band", "slab")
ORDER = ("slab", "band")
F32 = jnp.float32
BF16 = jnp.bfloat16
MIB = 1024 * 1024


def cos_sin(length):
    counter = np.arange(length)
    phases = (counter[:, None] * counter[None, :] % length) * (2.0 * math.pi / length)
    return np.cos(phases) / math.sqrt(length), np.sin(phases) / math.sqrt(length)


def bf16_table(values):
    return jnp.asarray(np.asarray(values, np.float32), dtype=BF16)


def x_order():
    x = np.arange(X).reshape(XB, BE // 2, 2)
    return x.transpose(2, 0, 1).reshape(-1)


def point_order():
    q = np.arange(P_SIZE).reshape(BE, BE, BE)
    return q.transpose(1, 0, 2).reshape(-1)


def nt(a, b):
    return lax.dot_general(a, b, (((1,), (1,)), ((), ())), preferred_element_type=F32)


def nn(a, b):
    return lax.dot_general(a, b, (((1,), (0,)), ((), ())), preferred_element_type=F32)


def two_stages(t, first, second, slots):
    def beside(now, before):
        one = first(now) if now is not None else ()
        two = second(before) if before is not None else ()
        for _ in zip_longest(one, two):
            pass

    pl.when(t == 0)(lambda: beside(slots[0], None))
    pl.when((t > 0) & (t < NSLAB) & (t % 2 == 0))(lambda: beside(slots[0], slots[1]))
    pl.when((t < NSLAB) & (t % 2 == 1))(lambda: beside(slots[1], slots[0]))
    pl.when(t == NSLAB)(lambda: beside(None, slots[(NSLAB - 1) % 2]))


def ahead(t):
    return jnp.minimum(t, NSLAB - 1)


def behind(t):
    return jnp.maximum(t - 1, 0)


def to_grid_kernel(spec_ref, ty_ref, tx_ref, out_ref, *slots):
    def along_y(across_ref):
        for e in range(0, BE, 2):
            across = []
            for i in range(2):
                plane = jnp.concatenate([spec_ref[0, 0, e + i], spec_ref[1, 0, e + i]], axis=1)
                across.append(nt(ty_ref[...], plane))
                if i == 0:
                    yield
            across = jnp.stack([a.reshape(2, NBAND, BE, X) for a in across], axis=2)
            across_ref[:, :, e // 2] = across.reshape(2, NBAND, 2 * BE, X).astype(BF16)
            yield

    def along_x(across_ref):
        low = lax.broadcasted_iota(jnp.int32, (X // 2, 128), 1) < HALF
        for c in range(0, NBAND, 2):
            re = [across_ref[0, c + i].reshape(BE * BE, X) for i in range(2)]
            im = [across_ref[1, c + i].reshape(BE * BE, X) for i in range(2)]
            whole = nt(tx_ref[0], jnp.concatenate([re[0], im[0], re[1], im[1]], axis=0)) + nt(
                tx_ref[1], jnp.concatenate([-im[0], re[0], -im[1], re[1]], axis=0)
            )
            for i in range(2):
                even = whole[: X // 2, i * 128 : (i + 1) * 128]
                odd = whole[X // 2 :, i * 128 : (i + 1) * 128]
                first = jnp.where(low, even, pltpu.roll(odd, HALF, 1))
                second = jnp.where(low, pltpu.roll(even, HALF, 1), odd)
                rows = jnp.stack(
                    [first.reshape(PAIRS, 8, 128), second.reshape(PAIRS, 8, 128)], axis=1
                ).reshape(X, 128)
                out_ref[0, c + i] = rows.astype(BF16)
            yield

    two_stages(pl.program_id(0), along_y, along_x, slots)


def to_grid(orbitals):
    cy, sy = cos_sin(Y)
    ty = bf16_table(np.block([[cy, -sy], [sy, cy]]))
    cx, sx = cos_sin(X)
    order = x_order()
    tx = bf16_table(np.stack([cx[order], sx[order]]))
    return pl.pallas_call(
        to_grid_kernel,
        grid=(NSLAB + 1,),
        in_specs=[
            pl.BlockSpec((2, 1, BE, X, Y), lambda t: (0, 0, ahead(t), 0, 0)),
            pl.BlockSpec((2 * Y, 2 * Y), lambda t: (0, 0)),
            pl.BlockSpec((2, X, X), lambda t: (0, 0, 0)),
        ],
        out_specs=pl.BlockSpec((1, NBAND, X, 128), lambda t: (behind(t), 0, 0, 0)),
        out_shape=pltpu.VMEM((NSLAB, NBAND, X, 128), BF16),
        scratch_shapes=[pltpu.VMEM((2, NBAND, BE // 2, 2 * BE, X), BF16)] * 2,
        compiler_params=pltpu.CompilerParams(vmem_limit_bytes=52 * MIB),
        name="to_grid",
    )(orbitals, ty, tx)


def turned_rows(bricks_ref, pair):
    turned = jnp.swapaxes(bricks_ref[:, pair * 16 : (pair + 1) * 16], 0, 1)
    return [
        jnp.concatenate(
            [
                jnp.concatenate([turned[part * 8 + low * 4 + high] for high in range(4)], axis=1)
                for part in range(2)
            ],
            axis=0,
        )
        for low in range(2)
    ]


def project_kernel(groups_ref, bricks_ref, natural_ref, turn_ref, proj_ref, sums_ref, coef_ref):
    t = pl.program_id(0)

    @pl.when(t == 0)
    def _():
        coef_ref[...] = jnp.zeros_like(coef_ref)

    for pair in range(PROJECT_STEP):
        rows = turned_rows(bricks_ref, pair)
        for low in range(2):
            b = 2 * pair + low
            proj_ref[b] = nn(natural_ref[b], turn_ref[...]).astype(BF16)
            partial = nt(proj_ref[b], rows[low])
            for k in range(KB):
                g = groups_ref[(2 * PROJECT_STEP * t + b) * KB + k]
                coef_ref[g] += partial[k * C : (k + 1) * C]

    @pl.when(t == PAIRS // PROJECT_STEP - 1)
    def _():
        sums_ref[...] = coef_ref[...].astype(BF16)


def project(groups, bricks, natural):
    turn = np.zeros((P_SIZE, P_SIZE))
    turn[point_order(), np.arange(P_SIZE)] = 1.0
    return pl.pallas_call(
        project_kernel,
        grid_spec=pltpu.PrefetchScalarGridSpec(
            num_scalar_prefetch=1,
            grid=(PAIRS // PROJECT_STEP,),
            in_specs=[
                pl.BlockSpec((NDEV, 16 * PROJECT_STEP, 128), lambda t, g: (0, t, 0)),
                pl.BlockSpec((2 * PROJECT_STEP, KB * C, P_SIZE), lambda t, g: (t, 0, 0)),
                pl.BlockSpec((P_SIZE, P_SIZE), lambda t, g: (0, 0)),
            ],
            out_specs=[
                pl.BlockSpec((2 * PROJECT_STEP, KB * C, P_SIZE), lambda t, g: (t, 0, 0)),
                pl.BlockSpec((NGROUP, C, ROWS), lambda t, g: (0, 0, 0)),
            ],
            scratch_shapes=[pltpu.VMEM((NGROUP, C, ROWS), F32)],
        ),
        out_shape=[
            jax.ShapeDtypeStruct((XB, KB * C, P_SIZE), BF16),
            jax.ShapeDtypeStruct((NGROUP, C, ROWS), BF16),
        ],
        compiler_params=pltpu.CompilerParams(vmem_limit_bytes=50 * MIB),
        name="project",
    )(groups, bricks, natural, bf16_table(turn))


def couple_kernel(sums_ref, strength_ref, out_ref):
    total = jnp.sum(sums_ref[...].astype(F32), axis=0)
    strength = 0.5 * (strength_ref[0] + strength_ref[0].T)
    scaled = strength[:, 0:1] * total[0:1]
    for j in range(1, PROJ):
        scaled = scaled + strength[:, j : j + 1] * total[j : j + 1]
    out_ref[...] = jnp.broadcast_to(scaled[None], (NDEV, PROJ, ROWS)).astype(BF16)


def couple(sums, strengths):
    return pl.pallas_call(
        couple_kernel,
        out_shape=jax.ShapeDtypeStruct((NDEV, PROJ, ROWS), BF16),
        compiler_params=pltpu.CompilerParams(vmem_limit_bytes=8 * MIB),
        name="couple",
    )(sums, strengths)


def act_kernel(groups_ref, coupled_ref, bricks_ref, proj_ref, pot_ref, out_ref, picks_ref):
    t = pl.program_id(0)

    @pl.when(t == 0)
    def _():
        unit = (
            lax.broadcasted_iota(jnp.int32, (ROWS, ROWS), 0)
            == lax.broadcasted_iota(jnp.int32, (ROWS, ROWS), 1)
        ).astype(BF16)
        zeros = jnp.zeros((C, ROWS), BF16)
        for g in range(NGROUP):
            block = coupled_ref[g]
            both = nt(unit, jnp.concatenate([block, zeros, zeros, block], axis=0)).astype(BF16)
            picks_ref[0, g] = both[:, : 2 * C]
            picks_ref[1, g] = both[:, 2 * C :]

    for pair in range(STEP):
        rows = turned_rows(bricks_ref, pair)
        pieces = [None] * 16
        for low in range(2):
            b = 2 * pair + low
            g = [groups_ref[(2 * STEP * t + b) * KB + k] for k in range(KB)]
            picked = jnp.concatenate(
                [picks_ref[0, g[0]] + picks_ref[1, g[1]], picks_ref[0, g[2]] + picks_ref[1, g[3]]],
                axis=1,
            )
            acted = nn(picked, proj_ref[b]) + pot_ref[b] * rows[low].astype(F32)
            acted = acted.astype(BF16)
            for part in range(2):
                for high in range(4):
                    pieces[part * 8 + low * 4 + high] = acted[
                        part * NDEV : (part + 1) * NDEV, high * 128 : (high + 1) * 128
                    ]
        out_ref[:, pair * 16 : (pair + 1) * 16] = jnp.swapaxes(jnp.stack(pieces), 0, 1)


def act(groups, coupled, bricks, proj, pot):
    return pl.pallas_call(
        act_kernel,
        grid_spec=pltpu.PrefetchScalarGridSpec(
            num_scalar_prefetch=1,
            grid=(PAIRS // STEP,),
            in_specs=[
                pl.BlockSpec((NGROUP, C, ROWS), lambda t, g: (0, 0, 0)),
                pl.BlockSpec((NDEV, 16 * STEP, 128), lambda t, g: (0, t, 0)),
                pl.BlockSpec((2 * STEP, KB * C, P_SIZE), lambda t, g: (t, 0, 0)),
                pl.BlockSpec((2 * STEP, 1, P_SIZE), lambda t, g: (t, 0, 0)),
            ],
            out_specs=pl.BlockSpec((NDEV, 16 * STEP, 128), lambda t, g: (0, t, 0)),
            scratch_shapes=[pltpu.VMEM((2, NGROUP, ROWS, 2 * C), BF16)],
        ),
        out_shape=pltpu.VMEM((NDEV, X, 128), BF16),
        compiler_params=pltpu.CompilerParams(vmem_limit_bytes=48 * MIB),
        name="act",
    )(groups, coupled, bricks, proj, pot)


def to_waves_kernel(
    grid_ref, spec_ref, below_ref, above_ref, tx_ref, ty_ref, planar_ref, out_ref, *slots
):
    t = pl.program_id(0)
    has_below = (t > 1).astype(F32)
    has_above = (t < NSLAB).astype(F32)

    def turn(turned_ref):
        for c in range(0, NBAND, 2):
            turned = [grid_ref[0, c + i].T.astype(F32).reshape(2, BE, 1, BE, X) for i in range(2)]
            turned = jnp.concatenate(turned, axis=2).reshape(2, BE, 2 * BE, X)
            turned_ref[:, :, c // 2] = turned.astype(BF16)
            yield

    def apply(turned_ref):
        for first in range(0, BE, PLANES):
            even = turned_ref[0, first : first + PLANES].reshape(PLANES * Y, X)
            odd = turned_ref[1, first : first + PLANES].reshape(PLANES * Y, X)
            even, odd = nt(tx_ref[0], even), nt(tx_ref[1], odd)
            front, back = even + odd, even - odd
            for i in range(PLANES):
                e = first + i
                cols = slice(i * Y, (i + 1) * Y)
                half = [
                    jnp.concatenate([front[o * HX : (o + 1) * HX, cols], back[o * HX : (o + 1) * HX, cols]], axis=0)
                    for o in range(2)
                ]
                half = jnp.concatenate(half, axis=1).astype(BF16)
                result = nn(half, ty_ref[...])
                for o in range(2):
                    here = spec_ref[o, 0, e].astype(F32)
                    if e == 0:
                        below = below_ref[o, 0, 0].astype(F32) * has_below
                    else:
                        below = spec_ref[o, 0, e - 1].astype(F32)
                    if e == BE - 1:
                        above = above_ref[o, 0, 0].astype(F32) * has_above
                    else:
                        above = spec_ref[o, 0, e + 1].astype(F32)
                    kinetic = planar_ref[...] * here - 0.5 * (above + below)
                    out_ref[o, 0, e] = (result[:, o * Y : (o + 1) * Y] + kinetic).astype(BF16)
                yield

    two_stages(t, turn, apply, slots)


def to_waves(grid, orbitals):
    cx, sx = cos_sin(X)
    x = np.arange(X).reshape(PAIRS, 2, BE // 2, 2)
    tables = []
    for low in range(2):
        own = x[..., low].reshape(PAIRS, 8)
        cos, sin = cx[:HX, own], sx[:HX, own]
        re, im = np.concatenate([cos, -sin]), np.concatenate([sin, cos])
        tables.append(np.stack([re, im], axis=2).reshape(X, X))
    tx = bf16_table(np.stack(tables))
    cy, sy = cos_sin(Y)
    ty = bf16_table(np.block([[cy, -sy], [sy, cy]]))
    wave_x = np.minimum(np.arange(X), X - np.arange(X)).astype(np.float32) / X
    wave_y = np.minimum(np.arange(Y), Y - np.arange(Y)).astype(np.float32) / Y
    planar = jnp.asarray(
        KINETIC_SCALE * (wave_x[:, None] * wave_x[:, None] + wave_y[None, :] * wave_y[None, :]) + 1.0, dtype=F32
    )
    return pl.pallas_call(
        to_waves_kernel,
        grid=(NSLAB + 1,),
        in_specs=[
            pl.BlockSpec((1, NBAND, X, 128), lambda t: (ahead(t), 0, 0, 0)),
            pl.BlockSpec((2, 1, BE, X, Y), lambda t: (0, 0, behind(t), 0, 0)),
            pl.BlockSpec((2, 1, 1, X, Y), lambda t: (0, 0, jnp.maximum(behind(t) * BE - 1, 0), 0, 0)),
            pl.BlockSpec((2, 1, 1, X, Y), lambda t: (0, 0, jnp.minimum(behind(t) * BE + BE, NZ - 1), 0, 0)),
            pl.BlockSpec((2, X, X), lambda t: (0, 0, 0)),
            pl.BlockSpec((2 * Y, 2 * Y), lambda t: (0, 0)),
            pl.BlockSpec((X, Y), lambda t: (0, 0)),
        ],
        out_specs=pl.BlockSpec((2, 1, BE, X, Y), lambda t: (0, 0, behind(t), 0, 0)),
        out_shape=jax.ShapeDtypeStruct((2, 1, NZ, X, Y), BF16),
        scratch_shapes=[pltpu.VMEM((2, BE, NBAND // 2, 2 * BE, X), BF16)] * 2,
        compiler_params=pltpu.CompilerParams(vmem_limit_bytes=48 * MIB),
        name="to_waves",
    )(grid, orbitals, orbitals, orbitals, tx, ty, planar)


def exchange(array):
    return lax.all_to_all(array, ORDER, split_axis=0, concat_axis=0, tiled=True)


def on_device(orbitals, potential, projector, block_group, strengths):
    groups = block_group.reshape(-1)
    strength = lax.dynamic_slice_in_dim(strengths, lax.axis_index(ORDER), 1, 0)
    grid, groups, strength = lax.optimization_barrier(
        (to_grid(orbitals).reshape(NDEV, X, 128), groups, strength)
    )
    bricks = exchange(grid)
    proj, sums = project(groups, bricks, projector.reshape(XB, KB * C, P_SIZE))
    sums, potential = lax.optimization_barrier((exchange(sums.reshape(NDEV, PROJ, ROWS)), potential))
    pot = potential.reshape(XB, BE, BE, BE).transpose(0, 2, 1, 3).reshape(XB, 1, P_SIZE)
    coupled = exchange(couple(sums, strength)).reshape(NGROUP, C, ROWS)
    coupled = pltpu.with_memory_space_constraint(coupled, pltpu.VMEM)
    acted = act(groups, coupled, bricks, proj, pot)
    returned = exchange(acted).reshape(NSLAB, NBAND, X, 128)
    return to_waves(returned, orbitals)


def solution(mesh):
    in_specs = (
        P(None, AXES, None, None, None),
        P("slab", None, "band", None),
        P("slab", None, "band", None, None, None),
        P("slab", None, "band", None),
        P(),
    )
    out_specs = P(None, AXES, None, None, None)
    return jax.shard_map(
        on_device, mesh=mesh, in_specs=in_specs, out_specs=out_specs, check_vma=False
    )
```
